32 devices in a mesh: dp: 4 (over y, x), fsdp: 8 (over z, core).
Axes of the slice: x: 2, y: 2, z: 4, core: 2. Of those that a mesh axis runs over, the one named last changes fastest.
Arguments:
- tokens: bfloat16 [16384, 8192], P(('dp', 'fsdp')), may hold values from -6 to 6
- cotangent: bfloat16 [16384, 1024], P(('dp', 'fsdp')), may hold values from -6 to 6
- weight: bfloat16 [8192, 1024], P('fsdp'), may hold values from -0.0625 to 0.0625
- feedback: float32 [4, 8192, 1024], P('dp', 'fsdp'), may hold values from -24 to 24
- q_factor: float32 [1024, 64], replicated, may hold values from -6 to 6
Outputs:
- input_grad: bfloat16 [16384, 8192], P(('dp', 'fsdp'))
- q_next: float32 [1024, 64], replicated
- feedback_next: float32 [4, 8192, 1024], P('dp', 'fsdp')
The draws below stay inside these ranges and needn't reach their ends.
All inputs are finite; a program needn't handle non-finite values.
Results may differ from the reference program's by a relative error of at most 0.012.
Values may be sent and summed in bfloat16 or wider, within the bound.
No kernel may reach another device: no remote copies, remote signals or barrier semaphores. Data moves between devices by JAX's collectives and lax.ppermute only.
A program may use at most 128 MiB of HBM per device.

```python
import jax
import jax.numpy as jnp
from jax import lax

D = 8192
KVW = 1024
RANK = 64
TOK_DEV = 512
GROUPS = 4
TOKENS = 16384
N_DP = 4
N_FSDP = 8


def draw_feedback(key, part):
    keys = jax.random.split(key, 3)
    position = jnp.arange(D, dtype=jnp.float32) / D
    rising = jnp.exp(jnp.log(3.0) * position)
    row_scale = jnp.exp(jax.random.uniform(keys[0], (D,), minval=jnp.log(0.3), maxval=0.0)) * rising
    col_scale = jnp.exp(jax.random.uniform(keys[1], (KVW,), minval=jnp.log(0.5), maxval=jnp.log(2.0)))
    base = jax.random.truncated_normal(keys[2], -4.0, 4.0, (GROUPS, D, KVW))
    return (base * row_scale[None, :, None] * col_scale[None, None, :]).astype(jnp.float32)


def block_scale(rng, extent, shards, low, largest):
    def one(dim, blocks):
        heights = jax.random.uniform(jax.random.fold_in(jax.random.fold_in(rng, 6), dim), (blocks,), jnp.float32, low / len(shards), largest / len(shards))
        return jnp.repeat(jnp.exp(heights), extent[dim] // blocks).reshape((-1,) + (1,) * (len(extent) - dim - 1))

    factor_of = one(*shards[0])
    for cut in shards[1:]:
        factor_of = factor_of * one(*cut)
    return factor_of


def centred(rng, shape, deviation, reach, shards=(), kind=jnp.bfloat16):
    array = jax.random.normal(rng, shape, jnp.float32) * deviation
    if len(shards) > 0:
        array = block_scale(rng, shape, shards, -0.22, 0.18) * array
    return jnp.clip(array, min=-reach, max=reach).astype(kind)


def setup_inputs(seed: int = 0) -> dict:
    arg_keys = jax.random.split(jax.random.key(seed), 6)
    tokens = centred(arg_keys[0], (TOKENS, D), 1.0, 6.0, ((0, 32),))
    cotangent = centred(arg_keys[1], (TOKENS, KVW), 1.0, 6.0, ((0, 32),))
    weight = centred(arg_keys[2], (D, KVW), D ** -0.5, 0.0625, ((0, 8),))
    feedback = draw_feedback(jax.random.fold_in(arg_keys[5], 71), 0)
    q_factor = centred(arg_keys[4], (KVW, RANK), 1.0, 6.0, (), jnp.float32)
    return dict(tokens=tokens, cotangent=cotangent, weight=weight, feedback=feedback, q_factor=q_factor)


highest = lax.Precision.HIGHEST

def reference(tokens, cotangent, weight, feedback, q_factor):
    cot_groups = cotangent.reshape(N_DP, N_FSDP * TOK_DEV, KVW)
    weight_wide = weight.astype(jnp.float32)

    def project(cot_block):
        product = lax.dot_general(cot_block.astype(jnp.float32), weight_wide, (((1,), (1,)), ((), ())), precision=highest)
        return product.astype(jnp.bfloat16)
    input_grad = lax.map(project, cot_groups).reshape(N_DP * N_FSDP * TOK_DEV, D)
    tok_blocks = tokens.reshape(N_DP, N_FSDP, TOK_DEV, D)
    cot_blocks = cotangent.reshape(N_DP, N_FSDP, TOK_DEV, KVW)

    def add_block(total, item):
        product = lax.dot_general(item[0].astype(jnp.float32), item[1].astype(jnp.float32), (((0,), (0,)), ((), ())), precision=highest)
        rounded = lax.optimization_barrier(product.astype(jnp.bfloat16))
        return (total + rounded.astype(jnp.float32), None)

    def group_grad(pair):
        total, _ = lax.scan(add_block, jnp.zeros((D, KVW), jnp.float32), pair)
        return total
    grad_scale = 1.0 / (TOK_DEV * N_FSDP) ** 0.5
    grads = lax.map(group_grad, (tok_blocks, cot_blocks)) * grad_scale
    merged = feedback + grads
    mean_merged = lax.optimization_barrier(jnp.mean(merged, axis=0))
    factor_p = jnp.dot(mean_merged, q_factor, precision=highest)
    gram_sum = jnp.dot(factor_p.T, factor_p, precision=highest)
    lower_factor = jnp.linalg.cholesky(gram_sum)
    p_hat = lax.linalg.triangular_solve(lower_factor, factor_p.T, left_side=True, lower=True).T
    q_next = jnp.dot(mean_merged.T, p_hat, precision=highest)
    feedback_next = merged - jnp.dot(p_hat, q_next.T, precision=highest)[None]
    return (input_grad, q_next, feedback_next)
```

```python
import math

import jax
import jax.numpy as jnp
from jax import lax
from jax.sharding import PartitionSpec as P

AXES = ("dp", "fsdp")
f32 = jnp.float32
bf16 = jnp.bfloat16
highest = lax.Precision.HIGHEST
high = lax.Precision.HIGH


def dot(left, right, dims, precision=None):
    return lax.dot_general(
        left, right, (dims, ((), ())), precision=precision, preferred_element_type=f32
    )


def halves(value):
    top = lax.reduce_precision(value, exponent_bits=8, mantissa_bits=7)
    return jnp.concatenate([top.astype(bf16), (value - top).astype(bf16)], axis=0)


def two_pass(left, right, dims):
    rows = left.shape[0]
    both = dot(halves(left), right, dims)
    return both[:rows] + both[rows:]


def per_device(tokens, cotangent, weight, feedback, q_factor):
    groups = lax.axis_size("dp")
    members = lax.axis_size("fsdp")
    chips = members // 2
    world = groups * members
    tok_dev, depth = tokens.shape
    rows, width = weight.shape
    d = lax.axis_index("dp")
    f = lax.axis_index("fsdp")
    flat = d * members + f
    z, c = f // 2, f % 2
    scale = 1.0 / math.sqrt(tok_dev * members)
    feedback = feedback[0]

    def swap(value, mask):
        return lax.ppermute(value, AXES, [(i, i ^ mask) for i in range(world)])

    def along(value, pairs):
        moves = [
            (g * members + a * 2 + core, g * members + b * 2 + core)
            for g in range(groups)
            for a, b in pairs
            for core in range(2)
        ]
        return lax.ppermute(value, AXES, moves)

    def bit(mask):
        return (flat // mask) % 2

    dp_masks = [members << i for i in range(groups.bit_length() - 1)]
    z_masks = [2 << i for i in range(chips.bit_length() - 1)]
    split_masks = [1] + dp_masks

    def split_sum(value, kind):
        for mask in split_masks:
            side, half = bit(mask), value.shape[1] // 2
            sent = lax.dynamic_slice_in_dim(value, (1 - side) * half, half, axis=1)
            kept = lax.dynamic_slice_in_dim(value, side * half, half, axis=1)
            sent = sent if mask == 1 else sent.astype(kind)
            value = kept + swap(sent, mask).astype(f32)
        for mask in z_masks:
            if kind == bf16:
                value = lax.reduce_precision(value, exponent_bits=8, mantissa_bits=7)
            value = value + swap(value.astype(kind), mask).astype(f32)
        return value

    def join(value):
        for mask in reversed(split_masks):
            other = swap(value, mask)
            value = jnp.where(
                bit(mask) == 0,
                jnp.concatenate([value, other], axis=1),
                jnp.concatenate([other, value], axis=1),
            )
        return value

    share = rows // groups
    piece = lax.dynamic_slice_in_dim(weight, d * share, share, axis=0)
    up, down = [piece], [piece]
    for _ in range(chips - 1):
        up.append(along(up[-1], [(a, a + 1) for a in range(chips - 1)]))
        down.append(along(down[-1], [(a + 1, a) for a in range(chips - 1)]))

    wide = tokens.reshape(tok_dev, chips, 2, rows)
    mine = lax.dynamic_index_in_dim(wide, c, axis=2, keepdims=False).reshape(tok_dev, -1)
    theirs = lax.dynamic_index_in_dim(wide, 1 - c, axis=2, keepdims=False).reshape(tok_dev, -1)
    chip_tokens = jnp.concatenate([mine, swap(theirs, 1)], axis=0)
    chip_cot = jnp.concatenate([cotangent, swap(cotangent, 1)], axis=0)

    chunks = 2
    tall = rows // chunks

    def part(block, j):
        left = lax.dynamic_slice_in_dim(chip_tokens, block * rows + j * tall, tall, axis=1)
        return dot(left, chip_cot, ((0,), (0,)))

    from_low, from_high = [None] * chunks, [None] * chunks

    def plus(value, *others):
        for other in others:
            if other is not None:
                value = value + other.astype(f32)
        return value

    for step in range(chips - 1):
        far = chips - 1 - step
        rising = [(a, a + 1) for a in range(step + 1)]
        falling = [(chips - 1 - a, chips - 2 - a) for a in range(step + 1)]
        for j in range(chunks):
            if step < far:
                block = jnp.where(z < chips // 2, z + far, z - far)
                block = jnp.clip(block, 0, chips - 1)
                extra = {id(x): x for x in (from_low[j], from_high[j])}.values()
                message = plus(part(block, j), *extra).astype(bf16)
                if step + 1 < far - 1:
                    from_low[j] = from_high[j] = along(message, rising + falling)
                else:
                    from_low[j] = along(message, rising)
                    from_high[j] = along(message, falling)
            else:
                upper = plus(part(jnp.minimum(z + far, chips - 1), j), from_low[j]).astype(bf16)
                lower = plus(part(jnp.maximum(z - far, 0), j), from_high[j]).astype(bf16)
                from_low[j] = along(upper, rising)
                from_high[j] = along(lower, falling)
    merged = [
        feedback[j * tall : (j + 1) * tall] + scale * plus(part(z, j), from_low[j], from_high[j])
        for j in range(chunks)
    ]

    cot_q = dot(q_factor, cotangent.astype(f32), ((0,), (1,)), highest) * scale
    p_part = two_pass(cot_q, tokens, ((1,), (0,)))
    p_rows = dot(q_factor, feedback, ((0,), (1,)), high)
    here = lax.dynamic_slice_in_dim(p_part, f * rows, rows, axis=1)
    p_part = lax.dynamic_update_slice_in_dim(p_part, here + p_rows, f * rows, axis=1)
    p_all = join(split_sum(p_part, bf16).astype(bf16))
    p_own = lax.dynamic_slice_in_dim(p_all, f * rows, rows, axis=1)

    tok_p = dot(p_all, tokens, ((1,), (1,)))
    z_part = two_pass(tok_p, cotangent, ((1,), (0,))) * scale
    z_part = z_part + dot(p_own.astype(f32), feedback, ((1,), (0,)), high)
    z_all = join(split_sum(z_part, f32))

    gram = dot(p_all, p_all, ((1,), (1,)))
    lower_factor = jnp.linalg.cholesky(gram)
    inverse = lax.linalg.triangular_solve(
        lower_factor, jnp.eye(gram.shape[0], dtype=f32), left_side=True, lower=True
    )
    hat_own = dot(inverse, p_own.astype(f32), ((1,), (0,)), highest)
    q_next = dot(inverse, z_all, ((1,), (0,)), highest) / groups
    feedback_next = jnp.concatenate(
        [
            merged[j] - dot(hat_own[:, j * tall : (j + 1) * tall], q_next, ((0,), (0,)), high)
            for j in range(chunks)
        ],
        axis=0,
    )

    slots = jnp.stack(
        [jnp.where(z + h < chips, down[h], up[chips - h]) for h in range(1, chips)]
    )
    shares = {0: slots}
    half = share // 2
    gathered = jnp.zeros((chips - 1, groups, share, width), bf16)
    gathered = lax.dynamic_update_slice(gathered, slots[:, None], (0, d, 0, 0))
    for m in range(1, groups):
        low_bit = m & -m
        high_bit = 1 << (m.bit_length() - 1)
        if low_bit == high_bit:
            shares[m] = swap(shares[m ^ low_bit], low_bit * members)
        else:
            first = swap(shares[m ^ low_bit][:, :half], low_bit * members)
            second = swap(shares[m ^ high_bit][:, half:], high_bit * members)
            shares[m] = jnp.concatenate([first, second], axis=1)
        gathered = lax.dynamic_update_slice(gathered, shares[m][:, None], (0, d ^ m, 0, 0))
    gathered = gathered.reshape(chips - 1, rows, width)
    other = swap(gathered, 1)
    input_grad = jnp.zeros((tok_dev, depth), bf16)

    def project(input_grad, block, shard):
        product = dot(cotangent, block, ((1,), (1,))).astype(bf16)
        return lax.dynamic_update_slice_in_dim(input_grad, product, shard * rows, axis=1)

    input_grad = project(input_grad, weight, f)
    input_grad = project(input_grad, swap(weight, 1), f ^ 1)
    for h in range(1, chips):
        chip = (z + h) % chips
        input_grad = project(input_grad, gathered[h - 1], chip * 2 + c)
        input_grad = project(input_grad, other[h - 1], chip * 2 + 1 - c)
    return (input_grad, q_next.T, feedback_next[None])


def solution(mesh):
    placed = (
        P(("dp", "fsdp"), None),
        P(("dp", "fsdp"), None),
        P("fsdp", None),
        P("dp", "fsdp", None),
        P(),
    )
    return jax.shard_map(
        per_device,
        mesh=mesh,
        in_specs=placed,
        out_specs=(P(("dp", "fsdp"), None), P(), P("dp", "fsdp", None)),
        check_vma=False,
    )
```

```python
import math

import jax
import jax.numpy as jnp
from jax import lax
from jax.experimental import pallas as pl
from jax.experimental.pallas import tpu as pltpu
from jax.sharding import PartitionSpec as P

AXES = ("dp", "fsdp")
f32 = jnp.float32
bf16 = jnp.bfloat16
highest = lax.Precision.HIGHEST
VMEM = 56 << 20


def cost(flops, moved):
    return pl.CostEstimate(flops=flops, bytes_accessed=moved, transcendentals=0)


def dot(left, right, dims, precision=None):
    return lax.dot_general(
        left, right, (dims, ((), ())), precision=precision, preferred_element_type=f32
    )


def crossed(left, right):
    return lax.dot_general(left, right, (((0,), (0,)), ((), ())), preferred_element_type=f32)


def times(left, right):
    return jnp.dot(left, right, preferred_element_type=f32)


def partials(c, start, tall, cot, other_cot, tokens, other, rows):
    tok, width = cot.shape
    chips = tokens.shape[1] // rows // 2
    tile = math.gcd(math.gcd(start, tall), min(512, rows // 2))
    steps = tall // tile

    def kernel(index, cot, other_cot, own, other, result):
        total = crossed(own[...], cot[...]) + crossed(other[...], other_cot[...])
        result[...] = total.astype(result.dtype)

    column = pl.BlockSpec(
        (tok, tile), lambda b, i, index: (0, (2 * b + index[0]) * (rows // tile) + start // tile + i)
    )
    return pl.pallas_call(
        kernel,
        grid_spec=pltpu.PrefetchScalarGridSpec(
            num_scalar_prefetch=1,
            grid=(chips, steps),
            in_specs=[whole(cot.shape), whole(other_cot.shape), column, column],
            out_specs=pl.BlockSpec((tile, width), lambda b, i, index: (b * steps + i, 0)),
        ),
        out_shape=jax.ShapeDtypeStruct((chips * tall, width), bf16),
        compiler_params=params(),
        cost_estimate=cost(4 * tok * width * tall * chips, 4 * chips * tall * (width + tok)),
    )(scalars(c), cot, other_cot, tokens, other)


def remove(feedback, hat, q):
    rows, width = feedback.shape
    rank = hat.shape[1]
    tile = rows // 2

    def kernel(feedback, hat, q, result):
        rank_part = jnp.dot(hat[...], q[...], precision=highest, preferred_element_type=f32)
        result[...] = feedback[...] - rank_part

    row = pl.BlockSpec((tile, width), lambda i: (i, 0))
    return pl.pallas_call(
        kernel,
        grid=(rows // tile,),
        in_specs=[row, pl.BlockSpec((tile, rank), lambda i: (i, 0)), whole(q.shape)],
        out_specs=row,
        out_shape=jax.ShapeDtypeStruct(feedback.shape, f32),
        compiler_params=params(),
        cost_estimate=cost(2 * rows * width * rank, 8 * rows * width),
    )(feedback, hat, q)


def finish(scale, start, gradient, base):
    tall, width = gradient.shape
    tile = math.gcd(start, tall)

    def kernel(gradient, base, result):
        result[...] = base[...] + scale * gradient[...].astype(f32)

    row = pl.BlockSpec((tile, width), lambda i: (start // tile + i, 0))
    return pl.pallas_call(
        kernel,
        grid=(tall // tile,),
        in_specs=[pl.BlockSpec((tile, width), lambda i: (i, 0)), row],
        out_specs=row,
        out_shape=jax.ShapeDtypeStruct(base.shape, f32),
        input_output_aliases={1: 0},
        compiler_params=params(),
        cost_estimate=cost(tall * width, 10 * tall * width),
    )(gradient, base)


def split(value):
    top = value.astype(bf16)
    return top, (value - top.astype(f32)).astype(bf16)


def scalars(*values):
    return jnp.stack([jnp.asarray(value, jnp.int32) for value in values])


def whole(shape):
    return pl.BlockSpec(shape, lambda *_: (0,) * len(shape))


def params():
    return pltpu.CompilerParams(vmem_limit_bytes=VMEM)


def left_part(scale, f, c, q_t, cot, tokens, feedback):
    rank, width = q_t.shape
    tok, depth = tokens.shape
    rows = feedback.shape[0]
    wide = 2 * rows
    half = depth // wide // 2

    def kernel(index, q_t, cot, tokens, feedback, sent, kept, factor):
        stage, j = pl.program_id(0), pl.program_id(1)
        side = jnp.where(stage == 0, 1 - index[1], index[1])

        @pl.when((stage == 0) & (j == 0))
        def _():
            top, low = split(q_t[...])
            nt = (((1,), (1,)), ((), ()))
            both = lax.dot_general(top, cot[...], nt, preferred_element_type=f32)
            both += lax.dot_general(low, cot[...], nt, preferred_element_type=f32)
            top, low = split(both * scale)
            factor[:rank] = top
            factor[rank:] = low

        both = times(factor[...], tokens[...])
        total = both[:rank] + both[rank:]
        mine = side * half + j == index[0] // 2
        column = pl.multiple_of(lax.rem(index[0], 2) * rows, 128)

        def store(ref):
            ref[...] = total.astype(ref.dtype)

            @pl.when(mine)
            def _():
                top, low = split(q_t[...])
                both = lax.dot_general(
                    jnp.concatenate([top, low], axis=0),
                    feedback[...].astype(bf16),
                    (((1,), (1,)), ((), ())),
                    preferred_element_type=f32,
                )
                here = ref[:, pl.ds(column, rows)].astype(f32)
                here += both[:rank] + both[rank:]
                ref[:, pl.ds(column, rows)] = here.astype(ref.dtype)

        @pl.when(stage == 0)
        def _():
            store(sent)

        @pl.when(stage == 1)
        def _():
            store(kept)

    def token_block(stage, j, index):
        return 0, jnp.where(stage == 0, 1 - index[1], index[1]) * half + j

    return pl.pallas_call(
        kernel,
        grid_spec=pltpu.PrefetchScalarGridSpec(
            num_scalar_prefetch=1,
            grid=(2, half),
            in_specs=[
                whole(q_t.shape),
                whole(cot.shape),
                pl.BlockSpec((tok, wide), token_block),
                whole(feedback.shape),
            ],
            out_specs=[
                pl.BlockSpec((rank, wide), lambda s, j, index: (0, jnp.where(s == 0, j, half - 1))),
                pl.BlockSpec((rank, wide), lambda s, j, index: (0, jnp.where(s == 0, 0, j))),
            ],
            scratch_shapes=[pltpu.VMEM((2 * rank, tok), bf16)],
        ),
        out_shape=[
            jax.ShapeDtypeStruct((rank, depth // 2), bf16),
            jax.ShapeDtypeStruct((rank, depth // 2), f32),
        ],
        compiler_params=params(),
        cost_estimate=cost(4 * rank * tok * depth, 2 * tok * depth + 4 * rows * width),
    )(scalars(f, c), q_t, cot, tokens, feedback)


def right_part(scale, f, c, p_all, tokens, cot, feedback):
    rank, depth = p_all.shape
    tok, width = cot.shape
    rows = feedback.shape[0]
    wide = 2 * rows
    steps = depth // wide
    half = width // 2

    def kernel(index, p_all, p_own, tokens, cot, feedback, sent, kept, total):
        step = pl.program_id(0)
        nt = (((1,), (1,)), ((), ()))
        term = lax.dot_general(p_all[...], tokens[...], nt, preferred_element_type=f32)

        @pl.when(step == 0)
        def _():
            total[...] = term

        @pl.when(step > 0)
        def _():
            total[...] += term

        @pl.when(step == steps - 1)
        def _():
            top, low = split(total[...])
            fb_top, fb_low = split(feedback[...])
            value = (times(top, cot[...]) + times(low, cot[...])) * scale
            value += times(p_own[...], fb_top) + times(p_own[...], fb_low)
            first, second = value[:, :half], value[:, half:]
            sent[...] = jnp.where(index[1] == 0, second, first)
            kept[...] = jnp.where(index[1] == 0, first, second)

    return pl.pallas_call(
        kernel,
        grid_spec=pltpu.PrefetchScalarGridSpec(
            num_scalar_prefetch=1,
            grid=(steps,),
            in_specs=[
                pl.BlockSpec((rank, wide), lambda i, index: (0, i)),
                pl.BlockSpec((rank, rows), lambda i, index: (0, index[0])),
                pl.BlockSpec((tok, wide), lambda i, index: (0, i)),
                whole(cot.shape),
                whole(feedback.shape),
            ],
            out_specs=[whole((rank, half))] * 2,
            scratch_shapes=[pltpu.VMEM((rank, tok), f32)],
        ),
        out_shape=[jax.ShapeDtypeStruct((rank, half), f32)] * 2,
        compiler_params=params(),
        cost_estimate=cost(2 * rank * tok * depth, 2 * tok * depth + 4 * rows * width),
    )(scalars(f, c), p_all, p_all, tokens, cot, feedback)


def on_core(function, side, shapes, *operands):
    if min(shape[-1] for shape, _ in shapes) % 128:
        return [x.astype(kind) for x, (_, kind) in zip(function(side, *operands), shapes)]

    def kernel(index, *refs):
        values = function(index[0], *[ref[...] for ref in refs[: len(operands)]])
        for ref, value in zip(refs[len(operands) :], values):
            ref[...] = value.astype(ref.dtype)

    return pl.pallas_call(
        kernel,
        grid_spec=pltpu.PrefetchScalarGridSpec(
            num_scalar_prefetch=1,
            grid=(1,),
            in_specs=[whole(x.shape) for x in operands],
            out_specs=[whole(shape) for shape, _ in shapes],
        ),
        out_shape=[jax.ShapeDtypeStruct(shape, kind) for shape, kind in shapes],
        compiler_params=params(),
        cost_estimate=cost(1, sum(x.size * x.dtype.itemsize for x in operands)),
    )(scalars(side), *operands)


def project_kernel(parts, table, cot, *refs):
    pieces = refs[: sum(parts)]
    result, token, tiles, sems = refs[-4:]
    step, steps = pl.program_id(0), pl.num_programs(0)
    slot = lax.rem(step, 2)
    wide = tiles.shape[3]

    def copy(k, slot, step):
        column = pl.multiple_of(table[step, k] * wide, 128)
        return pltpu.make_async_copy(
            tiles.at[slot, k], result.at[:, pl.ds(column, wide)], sems.at[slot, k]
        )

    @pl.when(step >= 2)
    def _():
        for k in range(len(parts)):
            copy(k, slot, step - 2).wait()

    at = 0
    for k, count in enumerate(parts):
        total, start = None, 0
        for piece in pieces[at : at + count]:
            depth = piece.shape[2]
            term = lax.dot_general(
                cot[:, start : start + depth],
                piece[0],
                (((1,), (1,)), ((), ())),
                preferred_element_type=f32,
            )
            total = term if total is None else total + term
            start += depth
        at += count
        tiles[slot, k] = total.astype(bf16)
        copy(k, slot, step).start()

    @pl.when(step == steps - 1)
    def _():
        token[...] = jnp.zeros(token.shape, token.dtype)
        for k in range(len(parts)):
            copy(k, slot, step).wait()

        @pl.when(steps > 1)
        def _():
            for k in range(len(parts)):
                copy(k, 1 - slot, step - 1).wait()


def project(result, depth, cot, pieces, table):
    count, wide, _ = pieces[0][0].shape
    tok, width = cot.shape
    if wide % 128:
        if result is None:
            result = jnp.zeros((tok, depth), bf16)
        for k, arrays in enumerate(pieces):
            full = jnp.concatenate(arrays, axis=2)
            for i in range(count):
                product = dot(cot, full[i], ((1,), (1,))).astype(bf16)
                result = lax.dynamic_update_slice_in_dim(
                    result, product, table[i, k] * wide, axis=1
                )
        return result, result[:8, :128].astype(f32)
    specs = [pl.BlockSpec((tok, width), lambda i, table: (0, 0))]
    operands = [table.astype(jnp.int32), cot]
    for arrays in pieces:
        for array in arrays:
            specs.append(pl.BlockSpec((1, wide, array.shape[2]), lambda i, table: (i, 0, 0)))
            operands.append(array)
    aliases = {}
    if result is not None:
        specs.append(pl.BlockSpec(memory_space=pl.ANY))
        aliases = {len(operands): 0}
        operands.append(result)
    parts = [len(arrays) for arrays in pieces]
    return pl.pallas_call(
        lambda *refs: project_kernel(parts, *refs),
        grid_spec=pltpu.PrefetchScalarGridSpec(
            num_scalar_prefetch=1,
            grid=(count,),
            in_specs=specs,
            out_specs=[pl.BlockSpec(memory_space=pl.ANY), whole((8, 128))],
            scratch_shapes=[
                pltpu.VMEM((2, len(parts), tok, wide), bf16),
                pltpu.SemaphoreType.DMA((2, len(parts))),
            ],
        ),
        out_shape=[jax.ShapeDtypeStruct((tok, depth), bf16), jax.ShapeDtypeStruct((8, 128), f32)],
        input_output_aliases=aliases,
        compiler_params=params(),
        cost_estimate=cost(2 * tok * width * wide * count * len(pieces), 2 * count * len(pieces) * wide * (width + tok)),
    )(*operands)


def per_device(tokens, cotangent, weight, feedback, q_factor):
    groups = lax.axis_size("dp")
    members = lax.axis_size("fsdp")
    chips = members // 2
    world = groups * members
    tok_dev, depth = tokens.shape
    rows, width = weight.shape
    d = lax.axis_index("dp")
    f = lax.axis_index("fsdp")
    flat = d * members + f
    z, c = f // 2, f % 2
    scale = 1.0 / math.sqrt(tok_dev * members)
    feedback = feedback[0]
    last = [None]

    def after(value):
        if last[0] is not None:
            value, _ = lax.optimization_barrier((value, last[0]))
        last[0] = value
        return value

    def gate(value):
        return lax.optimization_barrier((value, last[0]))[0]

    def swap(value, mask):
        return lax.ppermute(after(value), AXES, [(i, i ^ mask) for i in range(world)])

    def along(value, pairs):
        moves = [
            (g * members + a * 2 + core, g * members + b * 2 + core)
            for g in range(groups)
            for a, b in pairs
            for core in range(2)
        ]
        return lax.ppermute(after(value), AXES, moves)

    def paired(value, moves, odd=0):
        moves = [(a, b) for a, b in moves if (min(a, b) + odd) % 2 == 0]
        return along(value, moves) if moves else None

    results = {}

    def pick(index, parts):
        value = parts[0]
        for k in range(1, len(parts)):
            value = jnp.where(index == k, parts[k], value)
        return value

    def split_sum(sent, kept, kind):
        rank, wide = kept.shape
        got = swap(sent, 1)
        yield
        kept = gate(kept)
        wide //= groups

        def deal(place, kept, got):
            total = kept + got.astype(f32)
            parts = [total[:, k * wide : (k + 1) * wide] for k in range(groups)]
            return [pick(place ^ m, parts) for m in range(groups)]

        shapes = [((rank, wide), f32)] + [((rank, wide), kind)] * (groups - 1)
        kept, *sent = on_core(deal, d, shapes, kept, got)
        got = [swap(one, m * members) for m, one in enumerate(sent, 1)]
        yield
        kept = gate(kept)
        shapes = [((rank, wide), kind)]

        def add(_, kept, *got):
            for one in got:
                kept = kept + one.astype(f32)
            return [kept]

        (value,) = on_core(add, 0, shapes, kept, *got)
        terms = [swap(value, 2 * m) for m in range(1, chips)]
        yield
        terms = [gate(value)] + terms

        def pairs(_, *terms):
            terms = [term.astype(f32) for term in terms]
            while len(terms) > 1:
                terms = [a + b for a, b in zip(terms[::2], terms[1::2])]
            return terms

        return on_core(pairs, 0, shapes, *terms)[0]

    def join(value):
        for place, step, count in ((d, members, groups), (c, 1, 2)):
            others = [swap(value, m * step) for m in range(1, count)]
            yield
            value = gate(value)
            rank, wide = value.shape

            def beside(place, *terms, count=count):
                return [jnp.concatenate([pick(place ^ k, terms) for k in range(count)], axis=1)]

            shapes = [((rank, (count if wide % 128 == 0 else 1) * wide), value.dtype)]
            (value,) = on_core(beside, place, shapes, value, *others)
        return value

    def finish_of(generator):
        value = yield from generator
        return value

    other_cot, other = swap(cotangent, 1), swap(tokens, 1)

    def gradient():
        same_core = [[2 * a + core for a in range(chips)] for core in range(2)]
        parts = [(0, rows // 4), (rows // 4, rows - rows // 4)]
        summed = []
        for start, tall in parts:
            other_cot, other = results["other"]
            both = partials(c, start, tall, gate(cotangent), other_cot, tokens, other, rows)
            both = after(both)
            yield
            summed.append(
                lax.psum_scatter(
                    after(both), "fsdp", scatter_dimension=0, axis_index_groups=same_core, tiled=True
                )
            )
            yield
        result = results["low_rank"]
        for (start, _), part in zip(parts, summed):
            result = finish(scale, start, part, result)
            results["feedback"] = result
            yield

    def low_rank_chain():
        sent, kept = left_part(scale, f, c, q_factor.T, cotangent, tokens, feedback)
        sent = after(sent)
        results["other"] = after(other_cot), after(other)
        yield
        reduction = split_sum(sent, kept, bf16)
        p_sum = yield from reduction
        p_all = yield from join(p_sum)
        p_own = lax.dynamic_slice_in_dim(p_all, f * rows, rows, axis=1)
        z_part = right_part(scale, f, c, p_all, tokens, cotangent, feedback)
        reduction = split_sum(*z_part, f32)
        for _ in range(3):
            next(reduction)
            yield
        p_gated = gate(p_all)
        gram = dot(p_gated, p_gated, ((1,), (1,)))
        lower_factor = jnp.linalg.cholesky(gram)
        inverse = lax.linalg.triangular_solve(
            lower_factor, jnp.eye(gram.shape[0], dtype=f32), left_side=True, lower=True
        )
        inverse = after(inverse)
        yield
        z_sum = yield from finish_of(reduction)
        z_all = yield from join(z_sum)
        hat_own = dot(p_own.astype(f32), inverse, ((0,), (1,)), highest)
        q_next = dot(inverse, z_all, ((1,), (0,)), highest) / groups
        results["q_next"] = q_next.T
        results["low_rank"] = remove(feedback, hat_own, q_next)
        yield

    def weights():
        share = rows // groups
        piece = lax.dynamic_slice_in_dim(weight, d * share, share, axis=0)
        near, across = [piece], [piece]
        for h in range(chips - 1):
            moves = [(a, a + 1) for a in range(h, chips - 1)]
            moves += [(a + 1, a) for a in range(chips - 1 - h)]
            from_near, from_across = near[-1], across[-1]
            near.append(paired(from_across, moves))
            across.append(paired(from_near, moves, 1))
            if h == chips - 2:
                sibling = swap(weight, 1)
            yield
        toward = jnp.where(z % 2 == 0, 1, -1)
        count = jnp.where(z % 2 == 0, chips - 1 - z, z)
        slots, sources = [], []
        for k in range(1, chips):
            slot = near[k]
            for m in range(1, k, 2):
                slot = jnp.where(count == m, across[k - m], slot)
            slots.append(slot)
            sources.append(jnp.where(k <= count, z + toward * k, z - toward * (k - count)))
        slots, far = after(jnp.stack(slots)), jnp.stack(sources)
        yield
        shares, twins = {0: [slots]}, {}
        middle = width // 2
        for m in range(1, groups):
            low_bit = m & -m
            high_bit = 1 << (m.bit_length() - 1)
            if low_bit == high_bit:
                source = shares[m ^ low_bit]
                shares[m] = [swap(x, low_bit * members) for x in source]
                if m == 1:
                    twins[0] = [swap(slots, 1)]
            else:
                first = jnp.concatenate(shares[m ^ low_bit], axis=2)[:, :, :middle]
                second = jnp.concatenate(shares[m ^ high_bit], axis=2)[:, :, middle:]
                yield
                shares[m] = [
                    swap(first, low_bit * members),
                    swap(second, high_bit * members),
                ]
        for m in range(groups):
            if m not in twins and len(shares[m]) == 1:
                twins[m] = [swap(x, 1) for x in shares[m]]
        yield
        pieces = [[weight[None]], [sibling[None]]]
        result, token = project(
            None, depth, gate(cotangent), pieces, jnp.stack([f, f ^ 1])[None]
        )
        after(token)
        yield
        for m in range(groups):
            if m not in twins:
                twins[m] = [swap(x, 1) for x in shares[m]]
        pieces, table = [], []
        for m in range(groups):
            for core, arrays in ((c, shares[m]), (1 - c, twins[m])):
                pieces.append(arrays)
                table.append((far * 2 + core) * groups + (d ^ m))
        result, token = project(result, depth, gate(cotangent), pieces, jnp.stack(table, axis=1))
        results["input_grad"] = result
        after(token)
        yield

    chains = {"R": gradient(), "L": low_rank_chain(), "W": weights()}
    order = "WLWLLWLRWLRLLLRRLWLLWWLLW"
    for name in order:
        next(chains[name], None)
    for name in ("L", "W", "R"):
        for _ in chains[name]:
            pass
    return (results["input_grad"], results["q_next"], results["feedback"][None])


def solution(mesh):
    placed = (
        P(("dp", "fsdp"), None),
        P(("dp", "fsdp"), None),
        P("fsdp", None),
        P("dp", "fsdp", None),
        P(),
    )
    return jax.shard_map(
        per_device,
        mesh=mesh,
        in_specs=placed,
        out_specs=(P(("dp", "fsdp"), None), P(), P("dp", "fsdp", None)),
        check_vma=False,
    )
```

```python
import math

import jax
import jax.numpy as jnp
from jax import lax
from jax.experimental import pallas as pl
from jax.experimental.pallas import tpu as pltpu
from jax.sharding import PartitionSpec as P

AXES = ("dp", "fsdp")
f32 = jnp.float32
bf16 = jnp.bfloat16
highest = lax.Precision.HIGHEST
VMEM = 56 << 20


def cost(flops, moved):
    return pl.CostEstimate(flops=flops, bytes_accessed=moved, transcendentals=0)


def dot(left, right, dims, precision=None):
    return lax.dot_general(
        left, right, (dims, ((), ())), precision=precision, preferred_element_type=f32
    )


def crossed(left, right):
    return lax.dot_general(left, right, (((0,), (0,)), ((), ())), preferred_element_type=f32)


def times(left, right):
    return jnp.dot(left, right, preferred_element_type=f32)


def partials(c, start, tall, cot, other_cot, tokens, other, rows):
    tok, width = cot.shape
    chips = tokens.shape[1] // rows // 2
    tile = math.gcd(math.gcd(start, tall), min(512, rows // 2))
    steps = tall // tile

    def kernel(index, cot, other_cot, own, other, result):
        total = crossed(own[...], cot[...]) + crossed(other[...], other_cot[...])
        result[...] = total.astype(result.dtype)

    column = pl.BlockSpec(
        (tok, tile), lambda b, i, index: (0, (2 * b + index[0]) * (rows // tile) + start // tile + i)
    )
    return pl.pallas_call(
        kernel,
        grid_spec=pltpu.PrefetchScalarGridSpec(
            num_scalar_prefetch=1,
            grid=(chips, steps),
            in_specs=[whole(cot.shape), whole(other_cot.shape), column, column],
            out_specs=pl.BlockSpec((tile, width), lambda b, i, index: (b * steps + i, 0)),
        ),
        out_shape=jax.ShapeDtypeStruct((chips * tall, width), bf16),
        compiler_params=params(),
        cost_estimate=cost(4 * tok * width * tall * chips, 4 * chips * tall * (width + tok)),
    )(scalars(c), cot, other_cot, tokens, other)


def finish(scale, start, gradient, feedback, hat, q, result):
    tall, width = gradient.shape
    rank = hat.shape[1]
    tile = math.gcd(start, tall)
    tile = tile // 2 if tile > 512 else tile

    def kernel(gradient, feedback, hat, q, *refs):
        top, low = split(hat[...])
        q_top, q_low = split(q[...])
        rank_part = times(top, q_top) + (times(top, q_low) + times(low, q_top))
        refs[-1][...] = feedback[...] + (scale * gradient[...].astype(f32) - rank_part)

    row = pl.BlockSpec((tile, width), lambda i: (start // tile + i, 0))
    specs = [
        pl.BlockSpec((tile, width), lambda i: (i, 0)),
        row,
        pl.BlockSpec((tile, rank), lambda i: (start // tile + i, 0)),
        whole(q.shape),
    ]
    operands = [gradient, feedback, hat, q]
    aliases = {}
    if result is not None:
        specs.append(pl.BlockSpec(memory_space=pl.ANY))
        operands.append(result)
        aliases = {4: 0}
    return pl.pallas_call(
        kernel,
        grid=(tall // tile,),
        in_specs=specs,
        out_specs=row,
        out_shape=jax.ShapeDtypeStruct(feedback.shape, f32),
        input_output_aliases=aliases,
        compiler_params=params(),
        cost_estimate=cost(6 * rank * tall * width, 10 * tall * width),
    )(*operands)


def split(value):
    top = value.astype(bf16)
    return top, (value - top.astype(f32)).astype(bf16)


def scalars(*values):
    return jnp.stack([jnp.asarray(value, jnp.int32) for value in values])


def whole(shape):
    return pl.BlockSpec(shape, lambda *_: (0,) * len(shape))


def params():
    return pltpu.CompilerParams(vmem_limit_bytes=VMEM)


def left_factor(scale, core, q_t, cot, tokens, rows, kind):
    rank, width = q_t.shape
    tok, depth = tokens.shape
    steps = depth // rows // 4

    def kernel(index, q_t, cot, first, second, result, factor):
        @pl.when(pl.program_id(0) == 0)
        def _():
            top, low = split(q_t[...])
            nt = (((1,), (1,)), ((), ()))
            both = lax.dot_general(top, cot[...], nt, preferred_element_type=f32)
            both += lax.dot_general(low, cot[...], nt, preferred_element_type=f32)
            top, low = split(both * scale)
            factor[:rank] = top
            factor[rank:] = low

        for k, block in enumerate((first, second)):
            both = times(factor[...], block[...])
            result[:, k * rows : (k + 1) * rows] = (both[:rank] + both[rank:]).astype(kind)

    return pl.pallas_call(
        kernel,
        grid_spec=pltpu.PrefetchScalarGridSpec(
            num_scalar_prefetch=1,
            grid=(steps,),
            in_specs=[whole(q_t.shape), whole(cot.shape), *core_blocks(tok, rows)],
            out_specs=[
                pl.BlockSpec((rank, 2 * rows), lambda i, index: (0, i)),
                whole((2 * rank, tok)),
            ],
        ),
        out_shape=[
            jax.ShapeDtypeStruct((rank, depth // 2), kind),
            jax.ShapeDtypeStruct((2 * rank, tok), bf16),
        ],
        compiler_params=params(),
        cost_estimate=cost(2 * rank * tok * depth, tok * depth),
    )(scalars(core), q_t, cot, tokens, tokens)


def core_blocks(tok, rows):
    return [
        pl.BlockSpec((tok, rows), lambda i, index, k=k: (0, 4 * i + 2 * k + index[0]))
        for k in range(2)
    ]


def left_kept(core, chip, q_t, factor, tokens, feedback):
    rank, _ = q_t.shape
    tok, depth = tokens.shape
    rows = feedback.shape[0]
    steps = depth // rows // 4

    def kernel(index, q_t, factor, first, second, feedback, result):
        for k, block in enumerate((first, second)):
            both = times(factor[...], block[...])
            here = slice(k * rows, (k + 1) * rows)
            result[:, here] = both[:rank] + both[rank:]

            @pl.when(2 * pl.program_id(0) + k == index[1])
            def _():
                top, low = split(q_t[...])
                both = lax.dot_general(
                    jnp.concatenate([top, low], axis=0),
                    feedback[...].astype(bf16),
                    (((1,), (1,)), ((), ())),
                    preferred_element_type=f32,
                )
                result[:, here] += both[:rank] + both[rank:]

    return pl.pallas_call(
        kernel,
        grid_spec=pltpu.PrefetchScalarGridSpec(
            num_scalar_prefetch=1,
            grid=(steps,),
            in_specs=[
                whole(q_t.shape),
                whole(factor.shape),
                *core_blocks(tok, rows),
                whole(feedback.shape),
            ],
            out_specs=pl.BlockSpec((rank, 2 * rows), lambda i, index: (0, i)),
        ),
        out_shape=jax.ShapeDtypeStruct((rank, depth // 2), f32),
        compiler_params=params(),
        cost_estimate=cost(2 * rank * tok * depth, tok * depth + 4 * feedback.size),
    )(scalars(core, chip), q_t, factor, tokens, tokens, feedback)


def right_part(scale, chip, c, p_all, tokens, cot, feedback):
    rank, depth = p_all.shape
    tok, width = cot.shape
    rows = feedback.shape[0]
    wide = 2 * rows
    steps = depth // wide
    half = width // 2
    half_steps = steps // 2

    def block(i, k):
        return 4 * lax.rem(i, half_steps) + 2 * k + i // half_steps

    def kernel(index, p_all, p_own, first, second, cot, feedback, sent, kept, total):
        step = pl.program_id(0)
        nt = (((1,), (1,)), ((), ()))
        term = lax.dot_general(p_all[:, :rows], first[...], nt, preferred_element_type=f32)
        term += lax.dot_general(p_all[:, rows:], second[...], nt, preferred_element_type=f32)

        @pl.when(step == 0)
        def _():
            total[...] = term

        @pl.when(step > 0)
        def _():
            total[...] += term

        @pl.when(step == steps - 1)
        def _():
            top, low = split(total[...])
            fb_top, fb_low = split(feedback[...])
            value = (times(top, cot[...]) + times(low, cot[...])) * scale
            value += times(p_own[...], fb_top) + times(p_own[...], fb_low)
            first, second = value[:, :half], value[:, half:]
            sent[...] = jnp.where(index[1] == 0, second, first)
            kept[...] = jnp.where(index[1] == 0, first, second)

    return pl.pallas_call(
        kernel,
        grid_spec=pltpu.PrefetchScalarGridSpec(
            num_scalar_prefetch=1,
            grid=(steps,),
            in_specs=[
                pl.BlockSpec((rank, wide), lambda i, index: (0, i)),
                pl.BlockSpec((rank, rows), lambda i, index: (0, index[1] * 2 * half_steps + index[0])),
                *[
                    pl.BlockSpec((tok, rows), lambda i, index, k=k: (0, block(i, k)))
                    for k in range(2)
                ],
                whole(cot.shape),
                whole(feedback.shape),
            ],
            out_specs=[whole((rank, half))] * 2,
            scratch_shapes=[pltpu.VMEM((rank, tok), f32)],
        ),
        out_shape=[jax.ShapeDtypeStruct((rank, half), f32)] * 2,
        compiler_params=params(),
        cost_estimate=cost(2 * rank * tok * depth, 2 * tok * depth + 4 * rows * width),
    )(scalars(chip, c), p_all, p_all, tokens, tokens, cot, feedback)


def on_core(function, side, shapes, *operands):
    if min(shape[-1] for shape, _ in shapes) % 128:
        return [x.astype(kind) for x, (_, kind) in zip(function(side, *operands), shapes)]

    def kernel(index, *refs):
        values = function(index[0], *[ref[...] for ref in refs[: len(operands)]])
        for ref, value in zip(refs[len(operands) :], values):
            ref[...] = value.astype(ref.dtype)

    return pl.pallas_call(
        kernel,
        grid_spec=pltpu.PrefetchScalarGridSpec(
            num_scalar_prefetch=1,
            grid=(1,),
            in_specs=[whole(x.shape) for x in operands],
            out_specs=[whole(shape) for shape, _ in shapes],
        ),
        out_shape=[jax.ShapeDtypeStruct(shape, kind) for shape, kind in shapes],
        compiler_params=params(),
        cost_estimate=cost(1, sum(x.size * x.dtype.itemsize for x in operands)),
    )(scalars(side), *operands)


def project_kernel(parts, table, cot, *refs):
    pieces = refs[: sum(parts)]
    result, token, tiles, sems = refs[-4:]
    step, steps = pl.program_id(0), pl.num_programs(0)
    slot = lax.rem(step, 2)
    wide = tiles.shape[3]

    def copy(k, slot, step):
        column = pl.multiple_of(table[step, k] * wide, 128)
        return pltpu.make_async_copy(
            tiles.at[slot, k], result.at[:, pl.ds(column, wide)], sems.at[slot, k]
        )

    @pl.when(step >= 2)
    def _():
        for k in range(len(parts)):
            copy(k, slot, step - 2).wait()

    at = 0
    for k, count in enumerate(parts):
        total, start = None, 0
        for piece in pieces[at : at + count]:
            depth = piece.shape[2]
            term = lax.dot_general(
                cot[:, start : start + depth],
                piece[0],
                (((1,), (1,)), ((), ())),
                preferred_element_type=f32,
            )
            total = term if total is None else total + term
            start += depth
        at += count
        tiles[slot, k] = total.astype(bf16)
        copy(k, slot, step).start()

    @pl.when(step == steps - 1)
    def _():
        token[...] = jnp.zeros(token.shape, token.dtype)
        for k in range(len(parts)):
            copy(k, slot, step).wait()

        @pl.when(steps > 1)
        def _():
            for k in range(len(parts)):
                copy(k, 1 - slot, step - 1).wait()


def project(result, depth, cot, pieces, table):
    count, wide, _ = pieces[0][0].shape
    tok, width = cot.shape
    if wide % 128:
        if result is None:
            result = jnp.zeros((tok, depth), bf16)
        for k, arrays in enumerate(pieces):
            full = jnp.concatenate(arrays, axis=2)
            for i in range(count):
                product = dot(cot, full[i], ((1,), (1,))).astype(bf16)
                result = lax.dynamic_update_slice_in_dim(
                    result, product, table[i, k] * wide, axis=1
                )
        return result, jnp.zeros((8, 128), jnp.int32)
    specs = [pl.BlockSpec((tok, width), lambda i, table: (0, 0))]
    operands = [table.astype(jnp.int32), cot]
    for arrays in pieces:
        for array in arrays:
            specs.append(pl.BlockSpec((1, wide, array.shape[2]), lambda i, table: (i, 0, 0)))
            operands.append(array)
    aliases = {}
    if result is not None:
        specs.append(pl.BlockSpec(memory_space=pl.ANY))
        aliases = {len(operands): 0}
        operands.append(result)
    parts = [len(arrays) for arrays in pieces]
    return pl.pallas_call(
        lambda *refs: project_kernel(parts, *refs),
        grid_spec=pltpu.PrefetchScalarGridSpec(
            num_scalar_prefetch=1,
            grid=(count,),
            in_specs=specs,
            out_specs=[pl.BlockSpec(memory_space=pl.ANY), whole((8, 128))],
            scratch_shapes=[
                pltpu.VMEM((2, len(parts), tok, wide), bf16),
                pltpu.SemaphoreType.DMA((2, len(parts))),
            ],
        ),
        out_shape=[jax.ShapeDtypeStruct((tok, depth), bf16), jax.ShapeDtypeStruct((8, 128), jnp.int32)],
        input_output_aliases=aliases,
        compiler_params=params(),
        cost_estimate=cost(2 * tok * width * wide * count * len(pieces), 2 * count * len(pieces) * wide * (width + tok)),
    )(*operands)


def per_device(tokens, cotangent, weight, feedback, q_factor):
    groups = lax.axis_size("dp")
    members = lax.axis_size("fsdp")
    chips = members // 2
    world = groups * members
    tok_dev, depth = tokens.shape
    rows, width = weight.shape
    d = lax.axis_index("dp")
    f = lax.axis_index("fsdp")
    flat = d * members + f
    z, c = f // 2, f % 2
    scale = 1.0 / math.sqrt(tok_dev * members)
    feedback = feedback[0]
    last = [None]

    def after(value):
        if last[0] is not None:
            value, _ = lax.optimization_barrier((value, last[0]))
        last[0] = value
        return value

    def gate(value):
        return lax.optimization_barrier((value, last[0]))[0]

    def swap(value, mask):
        return lax.ppermute(after(value), AXES, [(i, i ^ mask) for i in range(world)])

    def along(value, pairs):
        moves = [
            (g * members + a * 2 + core, g * members + b * 2 + core)
            for g in range(groups)
            for a, b in pairs
            for core in range(2)
        ]
        return lax.ppermute(after(value), AXES, moves)

    def paired(value, moves, odd=0):
        moves = [(a, b) for a, b in moves if (min(a, b) + odd) % 2 == 0]
        return along(value, moves) if moves else None

    results = {}

    def pick(index, parts):
        value = parts[0]
        for k in range(1, len(parts)):
            value = jnp.where(index == k, parts[k], value)
        return value

    def split_sum(sent, kept, kind):
        rank, wide = kept.shape
        got = swap(sent, 1)
        yield
        kept = gate(kept)
        wide //= groups

        def deal(place, kept, got):
            total = kept + got.astype(f32)
            parts = [total[:, k * wide : (k + 1) * wide] for k in range(groups)]
            return [pick(place ^ m, parts) for m in range(groups)]

        shapes = [((rank, wide), f32)] + [((rank, wide), kind)] * (groups - 1)
        kept, *sent = on_core(deal, d, shapes, kept, got)
        got = [swap(one, m * members) for m, one in enumerate(sent, 1)]
        yield
        kept = gate(kept)
        shapes = [((rank, wide), kind)]

        def add(_, kept, *got):
            for one in got:
                kept = kept + one.astype(f32)
            return [kept]

        (value,) = on_core(add, 0, shapes, kept, *got)
        terms = [swap(value, 2 * m) for m in range(1, chips)]
        yield
        terms = [after(term) for term in terms]
        yield
        terms = [gate(value)] + terms

        def pairs(_, *terms):
            terms = [term.astype(f32) for term in terms]
            while len(terms) > 1:
                terms = [a + b for a, b in zip(terms[::2], terms[1::2])]
            return terms

        return on_core(pairs, 0, shapes, *terms)[0]

    def join(value):
        for place, step, count in ((d, members, groups), (c, 1, 2)):
            others = [swap(value, m * step) for m in range(1, count)]
            yield
            value = gate(value)
            rank, wide = value.shape

            def beside(place, *terms, count=count):
                return [jnp.concatenate([pick(place ^ k, terms) for k in range(count)], axis=1)]

            shapes = [((rank, (count if wide % 128 == 0 else 1) * wide), value.dtype)]
            (value,) = on_core(beside, place, shapes, value, *others)
        return value

    def finish_of(generator):
        value = yield from generator
        return value

    other_cot, other = swap(cotangent, 1), swap(tokens, 1)

    def gradient():
        same_core = [[2 * a + core for a in range(chips)] for core in range(2)]
        parts = [(rows - rows // 4, rows // 4), (0, rows - rows // 4)]
        summed = []
        for start, tall in parts:
            other_cot, other = results["other"]
            both = partials(c, start, tall, gate(cotangent), other_cot, tokens, other, rows)
            both = after(both)
            yield
            summed.append(
                lax.psum_scatter(
                    after(both), "fsdp", scatter_dimension=0, axis_index_groups=same_core, tiled=True
                )
            )
            yield
        hat, q = results["low_rank"]
        result = None
        for (start, _), part in zip(parts, summed):
            result = finish(scale, start, part, feedback, hat, q, result)
            results["feedback"] = result
            yield

    def low_rank_chain():
        q_t = q_factor.T
        sent, factor = left_factor(scale, 1 - c, q_t, cotangent, tokens, rows, bf16)
        sent = after(sent)
        results["other"] = after(other_cot), after(other)
        results["sibling"] = after(results["sibling"])
        yield
        kept = left_kept(c + results["zero"], z, q_t, factor, tokens, feedback)
        reduction = split_sum(sent, kept, bf16)
        p_sum = yield from reduction
        p_all = yield from join(p_sum)
        p_own = lax.dynamic_slice_in_dim(p_all, (c * chips + z) * rows, rows, axis=1)
        z_part = right_part(scale, z, c, p_all, tokens, cotangent, feedback)
        reduction = split_sum(*z_part, f32)
        for _ in range(2):
            next(reduction)
            yield
        p_gated = gate(p_all)
        gram = dot(p_gated, p_gated, ((1,), (1,)))
        lower_factor = jnp.linalg.cholesky(gram)
        inverse = lax.linalg.triangular_solve(
            lower_factor, jnp.eye(gram.shape[0], dtype=f32), left_side=True, lower=True
        )
        inverse = after(inverse)
        yield
        z_sum = yield from finish_of(reduction)
        z_all = yield from join(z_sum)
        hat_own = dot(p_own.astype(f32), inverse, ((0,), (1,)), highest)
        q_next = dot(inverse, z_all, ((1,), (0,)), highest) / groups
        results["q_next"] = q_next.T
        results["low_rank"] = hat_own, q_next
        yield

    def own_weights():
        results["sibling"] = swap(weight, 1)
        yield
        pieces = [[weight[None]], [results["sibling"][None]]]
        results["own"], token = project(
            None, depth, gate(cotangent), pieces, jnp.stack([f, f ^ 1])[None]
        )
        results["zero"] = token[0, 0]
        yield

    def weights():
        share = rows // groups
        piece = lax.dynamic_slice_in_dim(weight, d * share, share, axis=0)
        near, across = [piece], [piece]
        for h in range(chips - 1):
            moves = [(a, a + 1) for a in range(h, chips - 1)]
            moves += [(a + 1, a) for a in range(chips - 1 - h)]
            from_near, from_across = near[-1], across[-1]
            near.append(paired(from_across, moves))
            across.append(paired(from_near, moves, 1))
            yield
            if 0 < h < chips - 2:
                near[-1], across[-1] = after(near[-1]), after(across[-1])
                yield
        toward = jnp.where(z % 2 == 0, 1, -1)
        count = jnp.where(z % 2 == 0, chips - 1 - z, z)
        slots, sources = [], []
        for k in range(1, chips):
            slot = near[k]
            for m in range(1, k, 2):
                slot = jnp.where(count == m, across[k - m], slot)
            slots.append(slot)
            sources.append(jnp.where(k <= count, z + toward * k, z - toward * (k - count)))
        slots, far = after(jnp.stack(slots)), jnp.stack(sources)
        yield
        shares, twins = {0: [slots]}, {}
        middle = width // 2
        for m in range(1, groups):
            low_bit = m & -m
            high_bit = 1 << (m.bit_length() - 1)
            if low_bit == high_bit:
                source = shares[m ^ low_bit]
                shares[m] = [swap(x, low_bit * members) for x in source]
                if m == 1:
                    twins[0] = [swap(slots, 1)]
            else:
                first = jnp.concatenate(shares[m ^ low_bit], axis=2)[:, :, :middle]
                second = jnp.concatenate(shares[m ^ high_bit], axis=2)[:, :, middle:]
                yield
                shares[m] = [
                    swap(first, low_bit * members),
                    swap(second, high_bit * members),
                ]
        for m in range(groups):
            if m not in twins and len(shares[m]) == 1:
                twins[m] = [swap(x, 1) for x in shares[m]]
        yield
        for m in range(groups):
            if m not in twins:
                twins[m] = [swap(x, 1) for x in shares[m]]
        yield
        pieces, table = [], []
        for m in range(groups):
            for core, arrays in ((c, shares[m]), (1 - c, twins[m])):
                pieces.append(arrays)
                table.append((far * 2 + core) * groups + (d ^ m))
        results["input_grad"], _ = project(
            results["own"], depth, gate(cotangent), pieces, jnp.stack(table, axis=1)
        )
        yield

    chains = {"R": gradient(), "L": low_rank_chain(), "W": weights(), "O": own_weights()}
    order = "OWLWROWRLLLWRLWRLLWLLLLWLLWLLW"
    for name in order:
        next(chains[name], None)
    for name in "LWR":
        for _ in chains[name]:
            pass
    return (results["input_grad"], results["q_next"], results["feedback"][None])


def solution(mesh):
    placed = (
        P(("dp", "fsdp"), None),
        P(("dp", "fsdp"), None),
        P("fsdp", None),
        P("dp", "fsdp", None),
        P(),
    )
    return jax.shard_map(
        per_device,
        mesh=mesh,
        in_specs=placed,
        out_specs=(P(("dp", "fsdp"), None), P(), P("dp", "fsdp", None)),
        check_vma=False,
    )
```

```python
import math

import jax
import jax.numpy as jnp
from jax import lax
from jax.experimental import pallas as pl
from jax.experimental.pallas import tpu as pltpu
from jax.sharding import PartitionSpec as P

AXES = ("dp", "fsdp")
f32 = jnp.float32
bf16 = jnp.bfloat16
highest = lax.Precision.HIGHEST
VMEM = 56 << 20


def cost(flops, moved):
    return pl.CostEstimate(flops=flops, bytes_accessed=moved, transcendentals=0)


def dot(left, right, dims, precision=None):
    return lax.dot_general(
        left, right, (dims, ((), ())), precision=precision, preferred_element_type=f32
    )


def crossed(left, right):
    return lax.dot_general(left, right, (((0,), (0,)), ((), ())), preferred_element_type=f32)


def times(left, right):
    return jnp.dot(left, right, preferred_element_type=f32)


def partials(c, start, tall, cot, other_cot, tokens, other, rows):
    tok, width = cot.shape
    chips = tokens.shape[1] // rows // 2
    tile = math.gcd(math.gcd(start, tall), min(512, rows // 2))
    steps = tall // tile

    def kernel(index, cot, other_cot, own, other, result):
        total = crossed(own[...], cot[...]) + crossed(other[...], other_cot[...])
        result[...] = total.astype(result.dtype)

    column = pl.BlockSpec(
        (tok, tile), lambda b, i, index: (0, (2 * b + index[0]) * (rows // tile) + start // tile + i)
    )
    return pl.pallas_call(
        kernel,
        grid_spec=pltpu.PrefetchScalarGridSpec(
            num_scalar_prefetch=1,
            grid=(chips, steps),
            in_specs=[whole(cot.shape), whole(other_cot.shape), column, column],
            out_specs=pl.BlockSpec((tile, width), lambda b, i, index: (b * steps + i, 0)),
        ),
        out_shape=jax.ShapeDtypeStruct((chips * tall, width), bf16),
        compiler_params=params(),
        cost_estimate=cost(1, 1),
    )(scalars(c), cot, other_cot, tokens, other)


def finish(scale, start, gradient, feedback, hat, q, result):
    tall, width = gradient.shape
    rank = hat.shape[1]
    tile = math.gcd(start, tall)
    tile = tile // 2 if tile > 512 else tile

    def kernel(gradient, feedback, hat, q, *refs):
        top, low = split(hat[...])
        q_top, q_low = split(q[...])
        rank_part = times(top, q_top) + (times(top, q_low) + times(low, q_top))
        refs[-1][...] = feedback[...] + (scale * gradient[...].astype(f32) - rank_part)

    row = pl.BlockSpec((tile, width), lambda i: (start // tile + i, 0))
    specs = [
        pl.BlockSpec((tile, width), lambda i: (i, 0)),
        row,
        pl.BlockSpec((tile, rank), lambda i: (start // tile + i, 0)),
        whole(q.shape),
    ]
    operands = [gradient, feedback, hat, q]
    aliases = {}
    if result is not None:
        specs.append(pl.BlockSpec(memory_space=pl.ANY))
        operands.append(result)
        aliases = {4: 0}
    return pl.pallas_call(
        kernel,
        grid=(tall // tile,),
        in_specs=specs,
        out_specs=row,
        out_shape=jax.ShapeDtypeStruct(feedback.shape, f32),
        input_output_aliases=aliases,
        compiler_params=params(),
        cost_estimate=cost(6 * rank * tall * width, 10 * tall * width),
    )(*operands)


def split(value):
    top = value.astype(bf16)
    return top, (value - top.astype(f32)).astype(bf16)


def scalars(*values):
    return jnp.stack([jnp.asarray(value, jnp.int32) for value in values])


def whole(shape):
    return pl.BlockSpec(shape, lambda *_: (0,) * len(shape))


def params():
    return pltpu.CompilerParams(vmem_limit_bytes=VMEM)


def left_factor(scale, core, q_t, cot, tokens, rows, kind):
    rank, width = q_t.shape
    tok, depth = tokens.shape
    steps = depth // rows // 4

    def kernel(index, q_t, cot, first, second, result, factor):
        @pl.when(pl.program_id(0) == 0)
        def _():
            top, low = split(q_t[...])
            nt = (((1,), (1,)), ((), ()))
            both = lax.dot_general(top, cot[...], nt, preferred_element_type=f32)
            both += lax.dot_general(low, cot[...], nt, preferred_element_type=f32)
            top, low = split(both * scale)
            factor[:rank] = top
            factor[rank:] = low

        for k, block in enumerate((first, second)):
            both = times(factor[...], block[...])
            result[:, k * rows : (k + 1) * rows] = (both[:rank] + both[rank:]).astype(kind)

    return pl.pallas_call(
        kernel,
        grid_spec=pltpu.PrefetchScalarGridSpec(
            num_scalar_prefetch=1,
            grid=(steps,),
            in_specs=[whole(q_t.shape), whole(cot.shape), *core_blocks(tok, rows)],
            out_specs=[
                pl.BlockSpec((rank, 2 * rows), lambda i, index: (0, i)),
                whole((2 * rank, tok)),
            ],
        ),
        out_shape=[
            jax.ShapeDtypeStruct((rank, depth // 2), kind),
            jax.ShapeDtypeStruct((2 * rank, tok), bf16),
        ],
        compiler_params=params(),
        cost_estimate=cost(2 * rank * tok * depth, tok * depth),
    )(scalars(core), q_t, cot, tokens, tokens)


def core_blocks(tok, rows):
    return [
        pl.BlockSpec((tok, rows), lambda i, index, k=k: (0, 4 * i + 2 * k + index[0]))
        for k in range(2)
    ]


def left_kept(core, chip, q_t, factor, tokens, feedback):
    rank, _ = q_t.shape
    tok, depth = tokens.shape
    rows = feedback.shape[0]
    steps = depth // rows // 4

    def kernel(index, q_t, factor, first, second, feedback, result):
        for k, block in enumerate((first, second)):
            both = times(factor[...], block[...])
            here = slice(k * rows, (k + 1) * rows)
            result[:, here] = both[:rank] + both[rank:]

            @pl.when(2 * pl.program_id(0) + k == index[1])
            def _():
                top, low = split(q_t[...])
                both = lax.dot_general(
                    jnp.concatenate([top, low], axis=0),
                    feedback[...].astype(bf16),
                    (((1,), (1,)), ((), ())),
                    preferred_element_type=f32,
                )
                result[:, here] += both[:rank] + both[rank:]

    return pl.pallas_call(
        kernel,
        grid_spec=pltpu.PrefetchScalarGridSpec(
            num_scalar_prefetch=1,
            grid=(steps,),
            in_specs=[
                whole(q_t.shape),
                whole(factor.shape),
                *core_blocks(tok, rows),
                whole(feedback.shape),
            ],
            out_specs=pl.BlockSpec((rank, 2 * rows), lambda i, index: (0, i)),
        ),
        out_shape=jax.ShapeDtypeStruct((rank, depth // 2), f32),
        compiler_params=params(),
        cost_estimate=cost(2 * rank * tok * depth, tok * depth + 4 * feedback.size),
    )(scalars(core, chip), q_t, factor, tokens, tokens, feedback)


def right_part(scale, chip, c, p_all, tokens, cot, feedback):
    rank, depth = p_all.shape
    tok, width = cot.shape
    rows = feedback.shape[0]
    wide = 2 * rows
    steps = depth // wide
    half = width // 2
    half_steps = steps // 2

    def block(i, k):
        return 4 * lax.rem(i, half_steps) + 2 * k + i // half_steps

    def kernel(index, p_all, p_own, first, second, cot, feedback, sent, kept, total):
        step = pl.program_id(0)
        nt = (((1,), (1,)), ((), ()))
        term = lax.dot_general(p_all[:, :rows], first[...], nt, preferred_element_type=f32)
        term += lax.dot_general(p_all[:, rows:], second[...], nt, preferred_element_type=f32)

        @pl.when(step == 0)
        def _():
            total[...] = term

        @pl.when(step > 0)
        def _():
            total[...] += term

        @pl.when(step == steps - 1)
        def _():
            top, low = split(total[...])
            fb_top, fb_low = split(feedback[...])
            value = (times(top, cot[...]) + times(low, cot[...])) * scale
            value += times(p_own[...], fb_top) + times(p_own[...], fb_low)
            first, second = value[:, :half], value[:, half:]
            sent[...] = jnp.where(index[1] == 0, second, first)
            kept[...] = jnp.where(index[1] == 0, first, second)

    return pl.pallas_call(
        kernel,
        grid_spec=pltpu.PrefetchScalarGridSpec(
            num_scalar_prefetch=1,
            grid=(steps,),
            in_specs=[
                pl.BlockSpec((rank, wide), lambda i, index: (0, i)),
                pl.BlockSpec((rank, rows), lambda i, index: (0, index[1] * 2 * half_steps + index[0])),
                *[
                    pl.BlockSpec((tok, rows), lambda i, index, k=k: (0, block(i, k)))
                    for k in range(2)
                ],
                whole(cot.shape),
                whole(feedback.shape),
            ],
            out_specs=[whole((rank, half))] * 2,
            scratch_shapes=[pltpu.VMEM((rank, tok), f32)],
        ),
        out_shape=[jax.ShapeDtypeStruct((rank, half), f32)] * 2,
        compiler_params=params(),
        cost_estimate=cost(2 * rank * tok * depth, 2 * tok * depth + 4 * rows * width),
    )(scalars(chip, c), p_all, p_all, tokens, tokens, cot, feedback)


def on_core(function, side, shapes, *operands):
    if min(shape[-1] for shape, _ in shapes) % 128:
        return [x.astype(kind) for x, (_, kind) in zip(function(side, *operands), shapes)]

    def kernel(index, *refs):
        values = function(index[0], *[ref[...] for ref in refs[: len(operands)]])
        for ref, value in zip(refs[len(operands) :], values):
            ref[...] = value.astype(ref.dtype)

    return pl.pallas_call(
        kernel,
        grid_spec=pltpu.PrefetchScalarGridSpec(
            num_scalar_prefetch=1,
            grid=(1,),
            in_specs=[whole(x.shape) for x in operands],
            out_specs=[whole(shape) for shape, _ in shapes],
        ),
        out_shape=[jax.ShapeDtypeStruct(shape, kind) for shape, kind in shapes],
        compiler_params=params(),
        cost_estimate=cost(1, sum(x.size * x.dtype.itemsize for x in operands)),
    )(scalars(side), *operands)


def project_kernel(parts, table, cot, *refs):
    pieces = refs[: sum(parts)]
    result, token, tiles, sems = refs[-4:]
    step, steps = pl.program_id(0), pl.num_programs(0)
    slot = lax.rem(step, 2)
    wide = tiles.shape[3]

    def copy(k, slot, step):
        column = pl.multiple_of(table[step, k] * wide, 128)
        return pltpu.make_async_copy(
            tiles.at[slot, k], result.at[:, pl.ds(column, wide)], sems.at[slot, k]
        )

    @pl.when(step >= 2)
    def _():
        for k in range(len(parts)):
            copy(k, slot, step - 2).wait()

    at = 0
    for k, count in enumerate(parts):
        total, start = None, 0
        for piece in pieces[at : at + count]:
            depth = piece.shape[2]
            term = lax.dot_general(
                cot[:, start : start + depth],
                piece[0],
                (((1,), (1,)), ((), ())),
                preferred_element_type=f32,
            )
            total = term if total is None else total + term
            start += depth
        at += count
        tiles[slot, k] = total.astype(bf16)
        copy(k, slot, step).start()

    @pl.when(step == steps - 1)
    def _():
        token[...] = jnp.zeros(token.shape, token.dtype)
        for k in range(len(parts)):
            copy(k, slot, step).wait()

        @pl.when(steps > 1)
        def _():
            for k in range(len(parts)):
                copy(k, 1 - slot, step - 1).wait()


def project(result, depth, cot, pieces, table):
    count, wide, _ = pieces[0][0].shape
    tok, width = cot.shape
    if wide % 128:
        if result is None:
            result = jnp.zeros((tok, depth), bf16)
        for k, arrays in enumerate(pieces):
            full = jnp.concatenate(arrays, axis=2)
            for i in range(count):
                product = dot(cot, full[i], ((1,), (1,))).astype(bf16)
                result = lax.dynamic_update_slice_in_dim(
                    result, product, table[i, k] * wide, axis=1
                )
        return result, jnp.zeros((8, 128), jnp.int32)
    specs = [pl.BlockSpec((tok, width), lambda i, table: (0, 0))]
    operands = [table.astype(jnp.int32), cot]
    for arrays in pieces:
        for array in arrays:
            specs.append(pl.BlockSpec((1, wide, array.shape[2]), lambda i, table: (i, 0, 0)))
            operands.append(array)
    aliases = {}
    if result is not None:
        specs.append(pl.BlockSpec(memory_space=pl.ANY))
        aliases = {len(operands): 0}
        operands.append(result)
    parts = [len(arrays) for arrays in pieces]
    return pl.pallas_call(
        lambda *refs: project_kernel(parts, *refs),
        grid_spec=pltpu.PrefetchScalarGridSpec(
            num_scalar_prefetch=1,
            grid=(count,),
            in_specs=specs,
            out_specs=[pl.BlockSpec(memory_space=pl.ANY), whole((8, 128))],
            scratch_shapes=[
                pltpu.VMEM((2, len(parts), tok, wide), bf16),
                pltpu.SemaphoreType.DMA((2, len(parts))),
            ],
        ),
        out_shape=[jax.ShapeDtypeStruct((tok, depth), bf16), jax.ShapeDtypeStruct((8, 128), jnp.int32)],
        input_output_aliases=aliases,
        compiler_params=params(),
        cost_estimate=cost(2 * tok * width * wide * count * len(pieces), 2 * count * len(pieces) * wide * (width + tok)),
    )(*operands)


def per_device(tokens, cotangent, weight, feedback, q_factor):
    groups = lax.axis_size("dp")
    members = lax.axis_size("fsdp")
    chips = members // 2
    world = groups * members
    tok_dev, depth = tokens.shape
    rows, width = weight.shape
    d = lax.axis_index("dp")
    f = lax.axis_index("fsdp")
    flat = d * members + f
    z, c = f // 2, f % 2
    scale = 1.0 / math.sqrt(tok_dev * members)
    feedback = feedback[0]
    last = [None]

    def after(value):
        if last[0] is not None:
            value, _ = lax.optimization_barrier((value, last[0]))
        last[0] = value
        return value

    def gate(value):
        return lax.optimization_barrier((value, last[0]))[0]

    def swap(value, mask):
        return lax.ppermute(after(value), AXES, [(i, i ^ mask) for i in range(world)])

    def along(value, pairs):
        moves = [
            (g * members + a * 2 + core, g * members + b * 2 + core)
            for g in range(groups)
            for a, b in pairs
            for core in range(2)
        ]
        return lax.ppermute(after(value), AXES, moves)

    def paired(value, moves, odd=0):
        moves = [(a, b) for a, b in moves if (min(a, b) + odd) % 2 == 0]
        return along(value, moves) if moves else None

    results = {}

    def pick(index, parts):
        value = parts[0]
        for k in range(1, len(parts)):
            value = jnp.where(index == k, parts[k], value)
        return value

    def split_sum(sent, kept, kind):
        rank, wide = kept.shape
        got = swap(sent, 1)
        yield
        kept = gate(kept)
        wide //= groups

        def deal(place, kept, got):
            total = kept + got.astype(f32)
            parts = [total[:, k * wide : (k + 1) * wide] for k in range(groups)]
            return [pick(place ^ m, parts) for m in range(groups)]

        shapes = [((rank, wide), f32)] + [((rank, wide), kind)] * (groups - 1)
        kept, *sent = on_core(deal, d, shapes, kept, got)
        got = [swap(one, m * members) for m, one in enumerate(sent, 1)]
        yield
        kept = gate(kept)
        shapes = [((rank, wide), kind)]

        def add(_, kept, *got):
            for one in got:
                kept = kept + one.astype(f32)
            return [kept]

        (value,) = on_core(add, 0, shapes, kept, *got)
        terms = [swap(value, 2 * m) for m in range(1, chips)]
        yield
        terms = [after(term) for term in terms]
        yield
        terms = [gate(value)] + terms

        def pairs(_, *terms):
            terms = [term.astype(f32) for term in terms]
            while len(terms) > 1:
                terms = [a + b for a, b in zip(terms[::2], terms[1::2])]
            return terms

        return on_core(pairs, 0, shapes, *terms)[0]

    def join(value):
        for place, step, count in ((d, members, groups), (c, 1, 2)):
            others = [swap(value, m * step) for m in range(1, count)]
            yield
            value = gate(value)
            rank, wide = value.shape

            def beside(place, *terms, count=count):
                return [jnp.concatenate([pick(place ^ k, terms) for k in range(count)], axis=1)]

            shapes = [((rank, (count if wide % 128 == 0 else 1) * wide), value.dtype)]
            (value,) = on_core(beside, place, shapes, value, *others)
        return value

    def finish_of(generator):
        value = yield from generator
        return value

    other_cot, other = swap(cotangent, 1), swap(tokens, 1)

    def gradient():
        same_core = [[2 * a + core for a in range(chips)] for core in range(2)]
        parts = [(rows - rows // 4, rows // 4), (0, rows - rows // 4)]
        summed = []
        for start, tall in parts:
            other_cot, other = results["other"]
            both = partials(c, start, tall, gate(cotangent), other_cot, tokens, other, rows)
            both = after(both)
            yield
            summed.append(
                lax.psum_scatter(
                    after(both), "fsdp", scatter_dimension=0, axis_index_groups=same_core, tiled=True
                )
            )
            yield
        hat, q = results["low_rank"]
        result = None
        for (start, _), part in zip(parts, summed):
            result = finish(scale, start, part, feedback, hat, q, result)
            results["feedback"] = result
            yield

    def low_rank_chain():
        q_t = q_factor.T
        sent, factor = left_factor(scale, 1 - c, q_t, cotangent, tokens, rows, bf16)
        sent = after(sent)
        results["other"] = after(other_cot), after(other)
        results["sibling"] = after(results["sibling"])
        yield
        kept = left_kept(c + results["zero"], z, q_t, factor, tokens, feedback)
        reduction = split_sum(sent, kept, bf16)
        p_sum = yield from reduction
        p_all = yield from join(p_sum)
        p_own = lax.dynamic_slice_in_dim(p_all, (c * chips + z) * rows, rows, axis=1)
        z_part = right_part(scale, z, c, p_all, tokens, cotangent, feedback)
        reduction = split_sum(*z_part, f32)
        for _ in range(2):
            next(reduction)
            yield
        p_gated = gate(p_all)
        gram = dot(p_gated, p_gated, ((1,), (1,)))
        lower_factor = jnp.linalg.cholesky(gram)
        inverse = lax.linalg.triangular_solve(
            lower_factor, jnp.eye(gram.shape[0], dtype=f32), left_side=True, lower=True
        )
        inverse = after(inverse)
        yield
        z_sum = yield from finish_of(reduction)
        z_all = yield from join(z_sum)
        hat_own = dot(p_own.astype(f32), inverse, ((0,), (1,)), highest)
        q_next = dot(inverse, z_all, ((1,), (0,)), highest) / groups
        results["q_next"] = q_next.T
        results["low_rank"] = hat_own, q_next
        yield

    def own_weights():
        results["sibling"] = swap(weight, 1)
        yield
        pieces = [[weight[None]], [results["sibling"][None]]]
        results["own"], token = project(
            None, depth, gate(cotangent), pieces, jnp.stack([f, f ^ 1])[None]
        )
        results["zero"] = token[0, 0]
        yield

    def weights():
        share = rows // groups
        piece = lax.dynamic_slice_in_dim(weight, d * share, share, axis=0)
        near, across = [piece], [piece]
        for h in range(chips - 1):
            moves = [(a, a + 1) for a in range(h, chips - 1)]
            moves += [(a + 1, a) for a in range(chips - 1 - h)]
            from_near, from_across = near[-1], across[-1]
            near.append(paired(from_across, moves))
            across.append(paired(from_near, moves, 1))
            yield
            if 0 < h < chips - 2:
                near[-1], across[-1] = after(near[-1]), after(across[-1])
                yield
        near[-1] = after(near[-1])
        yield
        toward = jnp.where(z % 2 == 0, 1, -1)
        count = jnp.where(z % 2 == 0, chips - 1 - z, z)
        slots, sources = [], []
        for k in range(1, chips):
            slot = near[k]
            for m in range(1, k, 2):
                slot = jnp.where(count == m, across[k - m], slot)
            slots.append(slot)
            sources.append(jnp.where(k <= count, z + toward * k, z - toward * (k - count)))
        slots, far = after(jnp.stack(slots)), jnp.stack(sources)
        yield
        shares, twins = {0: [slots]}, {}
        middle = width // 2
        for m in range(1, groups):
            low_bit = m & -m
            high_bit = 1 << (m.bit_length() - 1)
            if low_bit == high_bit:
                source = shares[m ^ low_bit]
                shares[m] = [swap(x, low_bit * members) for x in source]
                if m == 1:
                    twins[0] = [swap(slots, 1)]
            else:
                first = jnp.concatenate(shares[m ^ low_bit], axis=2)[:, :, :middle]
                second = jnp.concatenate(shares[m ^ high_bit], axis=2)[:, :, middle:]
                yield
                shares[m] = [
                    swap(first, low_bit * members),
                    swap(second, high_bit * members),
                ]
        for m in range(groups):
            if m not in twins and len(shares[m]) == 1:
                twins[m] = [swap(x, 1) for x in shares[m]]
        yield
        for m in range(groups):
            if m not in twins:
                twins[m] = [swap(x, 1) for x in shares[m]]
        yield
        pieces, table = [], []
        for m in range(groups):
            for core, arrays in ((c, shares[m]), (1 - c, twins[m])):
                pieces.append(arrays)
                table.append((far * 2 + core) * groups + (d ^ m))
        results["input_grad"], _ = project(
            results["own"], depth, gate(cotangent), pieces, jnp.stack(table, axis=1)
        )
        yield

    chains = {"R": gradient(), "L": low_rank_chain(), "W": weights(), "O": own_weights()}
    order = "OWLWROWRWLLLRLWRWLLWLLLLWLLWLLW"
    for name in order:
        next(chains[name], None)
    for name in "LWR":
        for _ in chains[name]:
            pass
    return (results["input_grad"], results["q_next"], results["feedback"][None])


def solution(mesh):
    placed = (
        P(("dp", "fsdp"), None),
        P(("dp", "fsdp"), None),
        P("fsdp", None),
        P("dp", "fsdp", None),
        P(),
    )
    return jax.shard_map(
        per_device,
        mesh=mesh,
        in_specs=placed,
        out_specs=(P(("dp", "fsdp"), None), P(), P("dp", "fsdp", None)),
        check_vma=False,
    )
```

```python
import math

import jax
import jax.numpy as jnp
from jax import lax
from jax.experimental import pallas as pl
from jax.experimental.pallas import tpu as pltpu
from jax.sharding import PartitionSpec as P

AXES = ("dp", "fsdp")
f32 = jnp.float32
bf16 = jnp.bfloat16
highest = lax.Precision.HIGHEST
VMEM = 56 << 20


def cost(flops, moved):
    return pl.CostEstimate(flops=flops, bytes_accessed=moved, transcendentals=0)


def dot(left, right, dims, precision=None):
    return lax.dot_general(
        left, right, (dims, ((), ())), precision=precision, preferred_element_type=f32
    )


def crossed(left, right):
    return lax.dot_general(left, right, (((0,), (0,)), ((), ())), preferred_element_type=f32)


def times(left, right):
    return jnp.dot(left, right, preferred_element_type=f32)


def partials(c, start, tall, cot, other_cot, tokens, other, rows):
    tok, width = cot.shape
    chips = tokens.shape[1] // rows // 2
    tile = math.gcd(math.gcd(start, tall), min(512, rows // 2))
    steps = tall // tile

    def kernel(index, cot, other_cot, own, other, result):
        total = crossed(own[...], cot[...]) + crossed(other[...], other_cot[...])
        result[...] = total.astype(result.dtype)

    column = pl.BlockSpec(
        (tok, tile), lambda b, i, index: (0, (2 * b + index[0]) * (rows // tile) + start // tile + i)
    )
    return pl.pallas_call(
        kernel,
        grid_spec=pltpu.PrefetchScalarGridSpec(
            num_scalar_prefetch=1,
            grid=(chips, steps),
            in_specs=[whole(cot.shape), whole(other_cot.shape), column, column],
            out_specs=pl.BlockSpec((tile, width), lambda b, i, index: (b * steps + i, 0)),
        ),
        out_shape=jax.ShapeDtypeStruct((chips * tall, width), bf16),
        compiler_params=params(),
        cost_estimate=cost(1, 1),
    )(scalars(c), cot, other_cot, tokens, other)


def begin(scale, start, gradient, feedback, hat, q):
    tall, width = gradient.shape
    rows, rank = hat.shape
    tile = math.gcd(start, tall)
    first, count = start // tile, tall // tile

    def kernel(gradient, feedback, hat, q, result):
        top, low = split(hat[...])
        q_top, q_low = split(q[...])
        rank_part = times(top, q_top) + (times(top, q_low) + times(low, q_top))
        result[...] = feedback[...] - rank_part
        step = pl.program_id(0)

        @pl.when((step >= first) & (step < first + count))
        def _():
            result[...] += scale * gradient[...].astype(f32)

    row = pl.BlockSpec((tile, width), lambda i: (i, 0))
    return pl.pallas_call(
        kernel,
        grid=(rows // tile,),
        in_specs=[
            pl.BlockSpec((tile, width), lambda i: (jnp.clip(i - first, 0, count - 1), 0)),
            row,
            pl.BlockSpec((tile, rank), lambda i: (i, 0)),
            whole(q.shape),
        ],
        out_specs=row,
        out_shape=jax.ShapeDtypeStruct(feedback.shape, f32),
        compiler_params=params(),
        cost_estimate=cost(6 * rank * rows * width, 8 * rows * width),
    )(gradient, feedback, hat, q)


def finish(scale, start, gradient, base):
    tall, width = gradient.shape
    tile = math.gcd(start, tall)
    tile = tile // 2 if tile > 512 else tile

    def kernel(gradient, base, result):
        result[...] = base[...] + scale * gradient[...].astype(f32)

    row = pl.BlockSpec((tile, width), lambda i: (start // tile + i, 0))
    return pl.pallas_call(
        kernel,
        grid=(tall // tile,),
        in_specs=[pl.BlockSpec((tile, width), lambda i: (i, 0)), row],
        out_specs=row,
        out_shape=jax.ShapeDtypeStruct(base.shape, f32),
        input_output_aliases={1: 0},
        compiler_params=params(),
        cost_estimate=cost(tall * width, 10 * tall * width),
    )(gradient, base)


def split(value):
    top = value.astype(bf16)
    return top, (value - top.astype(f32)).astype(bf16)


def scalars(*values):
    return jnp.stack([jnp.asarray(value, jnp.int32) for value in values])


def whole(shape):
    return pl.BlockSpec(shape, lambda *_: (0,) * len(shape))


def params():
    return pltpu.CompilerParams(vmem_limit_bytes=VMEM)


def left_factor(scale, core, q_t, cot, tokens, rows, kind):
    rank, width = q_t.shape
    tok, depth = tokens.shape
    steps = depth // rows // 4

    def kernel(index, q_t, cot, first, second, result, factor):
        @pl.when(pl.program_id(0) == 0)
        def _():
            top, low = split(q_t[...])
            nt = (((1,), (1,)), ((), ()))
            both = lax.dot_general(top, cot[...], nt, preferred_element_type=f32)
            both += lax.dot_general(low, cot[...], nt, preferred_element_type=f32)
            top, low = split(both * scale)
            factor[:rank] = top
            factor[rank:] = low

        for k, block in enumerate((first, second)):
            both = times(factor[...], block[...])
            result[:, k * rows : (k + 1) * rows] = (both[:rank] + both[rank:]).astype(kind)

    return pl.pallas_call(
        kernel,
        grid_spec=pltpu.PrefetchScalarGridSpec(
            num_scalar_prefetch=1,
            grid=(steps,),
            in_specs=[whole(q_t.shape), whole(cot.shape), *core_blocks(tok, rows)],
            out_specs=[
                pl.BlockSpec((rank, 2 * rows), lambda i, index: (0, i)),
                whole((2 * rank, tok)),
            ],
        ),
        out_shape=[
            jax.ShapeDtypeStruct((rank, depth // 2), kind),
            jax.ShapeDtypeStruct((2 * rank, tok), bf16),
        ],
        compiler_params=params(),
        cost_estimate=cost(2 * rank * tok * depth, tok * depth),
    )(scalars(core), q_t, cot, tokens, tokens)


def core_blocks(tok, rows):
    return [
        pl.BlockSpec((tok, rows), lambda i, index, k=k: (0, 4 * i + 2 * k + index[0]))
        for k in range(2)
    ]


def left_kept(core, chip, q_t, factor, tokens, feedback):
    rank, _ = q_t.shape
    tok, depth = tokens.shape
    rows = feedback.shape[0]
    steps = depth // rows // 4

    def kernel(index, q_t, factor, first, second, feedback, result):
        for k, block in enumerate((first, second)):
            both = times(factor[...], block[...])
            here = slice(k * rows, (k + 1) * rows)
            result[:, here] = both[:rank] + both[rank:]

            @pl.when(2 * pl.program_id(0) + k == index[1])
            def _():
                top, low = split(q_t[...])
                both = lax.dot_general(
                    jnp.concatenate([top, low], axis=0),
                    feedback[...].astype(bf16),
                    (((1,), (1,)), ((), ())),
                    preferred_element_type=f32,
                )
                result[:, here] += both[:rank] + both[rank:]

    return pl.pallas_call(
        kernel,
        grid_spec=pltpu.PrefetchScalarGridSpec(
            num_scalar_prefetch=1,
            grid=(steps,),
            in_specs=[
                whole(q_t.shape),
                whole(factor.shape),
                *core_blocks(tok, rows),
                whole(feedback.shape),
            ],
            out_specs=pl.BlockSpec((rank, 2 * rows), lambda i, index: (0, i)),
        ),
        out_shape=jax.ShapeDtypeStruct((rank, depth // 2), f32),
        compiler_params=params(),
        cost_estimate=cost(2 * rank * tok * depth, tok * depth + 4 * feedback.size),
    )(scalars(core, chip), q_t, factor, tokens, tokens, feedback)


def right_part(scale, chip, c, p_all, tokens, cot, feedback):
    rank, depth = p_all.shape
    tok, width = cot.shape
    rows = feedback.shape[0]
    wide = 2 * rows
    steps = depth // wide
    half = width // 2
    half_steps = steps // 2

    def block(i, k):
        return 4 * lax.rem(i, half_steps) + 2 * k + i // half_steps

    def kernel(index, p_all, p_own, first, second, cot, feedback, sent, kept, total):
        step = pl.program_id(0)
        nt = (((1,), (1,)), ((), ()))
        term = lax.dot_general(p_all[:, :rows], first[...], nt, preferred_element_type=f32)
        term += lax.dot_general(p_all[:, rows:], second[...], nt, preferred_element_type=f32)

        @pl.when(step == 0)
        def _():
            total[...] = term

        @pl.when(step > 0)
        def _():
            total[...] += term

        @pl.when(step == steps - 1)
        def _():
            top, low = split(total[...])
            fb_top, fb_low = split(feedback[...])
            value = (times(top, cot[...]) + times(low, cot[...])) * scale
            value += times(p_own[...], fb_top) + times(p_own[...], fb_low)
            first, second = value[:, :half], value[:, half:]
            sent[...] = jnp.where(index[1] == 0, second, first)
            kept[...] = jnp.where(index[1] == 0, first, second)

    return pl.pallas_call(
        kernel,
        grid_spec=pltpu.PrefetchScalarGridSpec(
            num_scalar_prefetch=1,
            grid=(steps,),
            in_specs=[
                pl.BlockSpec((rank, wide), lambda i, index: (0, i)),
                pl.BlockSpec((rank, rows), lambda i, index: (0, index[1] * 2 * half_steps + index[0])),
                *[
                    pl.BlockSpec((tok, rows), lambda i, index, k=k: (0, block(i, k)))
                    for k in range(2)
                ],
                whole(cot.shape),
                whole(feedback.shape),
            ],
            out_specs=[whole((rank, half))] * 2,
            scratch_shapes=[pltpu.VMEM((rank, tok), f32)],
        ),
        out_shape=[jax.ShapeDtypeStruct((rank, half), f32)] * 2,
        compiler_params=params(),
        cost_estimate=cost(2 * rank * tok * depth, 2 * tok * depth + 4 * rows * width),
    )(scalars(chip, c), p_all, p_all, tokens, tokens, cot, feedback)


def on_core(function, side, shapes, *operands):
    if min(shape[-1] for shape, _ in shapes) % 128:
        return [x.astype(kind) for x, (_, kind) in zip(function(side, *operands), shapes)]

    def kernel(index, *refs):
        values = function(index[0], *[ref[...] for ref in refs[: len(operands)]])
        for ref, value in zip(refs[len(operands) :], values):
            ref[...] = value.astype(ref.dtype)

    return pl.pallas_call(
        kernel,
        grid_spec=pltpu.PrefetchScalarGridSpec(
            num_scalar_prefetch=1,
            grid=(1,),
            in_specs=[whole(x.shape) for x in operands],
            out_specs=[whole(shape) for shape, _ in shapes],
        ),
        out_shape=[jax.ShapeDtypeStruct(shape, kind) for shape, kind in shapes],
        compiler_params=params(),
        cost_estimate=cost(1, sum(x.size * x.dtype.itemsize for x in operands)),
    )(scalars(side), *operands)


def project_kernel(parts, table, cot, *refs):
    pieces = refs[: sum(parts)]
    result, token, tiles, sems = refs[-4:]
    step, steps = pl.program_id(0), pl.num_programs(0)
    slot = lax.rem(step, 2)
    wide = tiles.shape[3]

    def copy(k, slot, step):
        column = pl.multiple_of(table[step, k] * wide, 128)
        return pltpu.make_async_copy(
            tiles.at[slot, k], result.at[:, pl.ds(column, wide)], sems.at[slot, k]
        )

    @pl.when(step >= 2)
    def _():
        for k in range(len(parts)):
            copy(k, slot, step - 2).wait()

    at = 0
    for k, count in enumerate(parts):
        total, start = None, 0
        for piece in pieces[at : at + count]:
            depth = piece.shape[2]
            term = lax.dot_general(
                cot[:, start : start + depth],
                piece[0],
                (((1,), (1,)), ((), ())),
                preferred_element_type=f32,
            )
            total = term if total is None else total + term
            start += depth
        at += count
        tiles[slot, k] = total.astype(bf16)
        copy(k, slot, step).start()

    @pl.when(step == steps - 1)
    def _():
        token[...] = jnp.zeros(token.shape, token.dtype)
        for k in range(len(parts)):
            copy(k, slot, step).wait()

        @pl.when(steps > 1)
        def _():
            for k in range(len(parts)):
                copy(k, 1 - slot, step - 1).wait()


def project(result, depth, cot, pieces, table):
    count, wide, _ = pieces[0][0].shape
    tok, width = cot.shape
    if wide % 128:
        if result is None:
            result = jnp.zeros((tok, depth), bf16)
        for k, arrays in enumerate(pieces):
            full = jnp.concatenate(arrays, axis=2)
            for i in range(count):
                product = dot(cot, full[i], ((1,), (1,))).astype(bf16)
                result = lax.dynamic_update_slice_in_dim(
                    result, product, table[i, k] * wide, axis=1
                )
        return result, jnp.zeros((8, 128), jnp.int32)
    specs = [pl.BlockSpec((tok, width), lambda i, table: (0, 0))]
    operands = [table.astype(jnp.int32), cot]
    for arrays in pieces:
        for array in arrays:
            specs.append(pl.BlockSpec((1, wide, array.shape[2]), lambda i, table: (i, 0, 0)))
            operands.append(array)
    aliases = {}
    if result is not None:
        specs.append(pl.BlockSpec(memory_space=pl.ANY))
        aliases = {len(operands): 0}
        operands.append(result)
    parts = [len(arrays) for arrays in pieces]
    return pl.pallas_call(
        lambda *refs: project_kernel(parts, *refs),
        grid_spec=pltpu.PrefetchScalarGridSpec(
            num_scalar_prefetch=1,
            grid=(count,),
            in_specs=specs,
            out_specs=[pl.BlockSpec(memory_space=pl.ANY), whole((8, 128))],
            scratch_shapes=[
                pltpu.VMEM((2, len(parts), tok, wide), bf16),
                pltpu.SemaphoreType.DMA((2, len(parts))),
            ],
        ),
        out_shape=[jax.ShapeDtypeStruct((tok, depth), bf16), jax.ShapeDtypeStruct((8, 128), jnp.int32)],
        input_output_aliases=aliases,
        compiler_params=params(),
        cost_estimate=cost(2 * tok * width * wide * count * len(pieces), 2 * count * len(pieces) * wide * (width + tok)),
    )(*operands)


def per_device(tokens, cotangent, weight, feedback, q_factor):
    groups = lax.axis_size("dp")
    members = lax.axis_size("fsdp")
    chips = members // 2
    world = groups * members
    tok_dev, depth = tokens.shape
    rows, width = weight.shape
    d = lax.axis_index("dp")
    f = lax.axis_index("fsdp")
    flat = d * members + f
    z, c = f // 2, f % 2
    scale = 1.0 / math.sqrt(tok_dev * members)
    feedback = feedback[0]
    last = [None]

    def after(value):
        if last[0] is not None:
            value, _ = lax.optimization_barrier((value, last[0]))
        last[0] = value
        return value

    def gate(value):
        return lax.optimization_barrier((value, last[0]))[0]

    def swap(value, mask):
        return lax.ppermute(after(value), AXES, [(i, i ^ mask) for i in range(world)])

    def along(value, pairs):
        moves = [
            (g * members + a * 2 + core, g * members + b * 2 + core)
            for g in range(groups)
            for a, b in pairs
            for core in range(2)
        ]
        return lax.ppermute(after(value), AXES, moves)

    def paired(value, moves, odd=0):
        moves = [(a, b) for a, b in moves if (min(a, b) + odd) % 2 == 0]
        return along(value, moves) if moves else None

    results = {}

    def pick(index, parts):
        value = parts[0]
        for k in range(1, len(parts)):
            value = jnp.where(index == k, parts[k], value)
        return value

    def split_sum(sent, kept, kind):
        rank, wide = kept.shape
        got = swap(sent, 1)
        yield
        kept = gate(kept)
        wide //= groups

        def deal(place, kept, got):
            total = kept + got.astype(f32)
            parts = [total[:, k * wide : (k + 1) * wide] for k in range(groups)]
            return [pick(place ^ m, parts) for m in range(groups)]

        shapes = [((rank, wide), f32)] + [((rank, wide), kind)] * (groups - 1)
        kept, *sent = on_core(deal, d, shapes, kept, got)
        got = [swap(one, m * members) for m, one in enumerate(sent, 1)]
        yield
        kept = gate(kept)
        shapes = [((rank, wide), kind)]

        def add(_, kept, *got):
            for one in got:
                kept = kept + one.astype(f32)
            return [kept]

        (value,) = on_core(add, 0, shapes, kept, *got)
        terms = [swap(value, 2 * m) for m in range(1, chips)]
        yield
        terms = [after(term) for term in terms]
        yield
        terms = [gate(value)] + terms

        def pairs(_, *terms):
            terms = [term.astype(f32) for term in terms]
            while len(terms) > 1:
                terms = [a + b for a, b in zip(terms[::2], terms[1::2])]
            return terms

        return on_core(pairs, 0, shapes, *terms)[0]

    def join(value):
        for place, step, count in ((d, members, groups), (c, 1, 2)):
            others = [swap(value, m * step) for m in range(1, count)]
            yield
            value = gate(value)
            rank, wide = value.shape

            def beside(place, *terms, count=count):
                return [jnp.concatenate([pick(place ^ k, terms) for k in range(count)], axis=1)]

            shapes = [((rank, (count if wide % 128 == 0 else 1) * wide), value.dtype)]
            (value,) = on_core(beside, place, shapes, value, *others)
        return value

    def finish_of(generator):
        value = yield from generator
        return value

    other_cot, other = swap(cotangent, 1), swap(tokens, 1)

    def gradient():
        same_core = [[2 * a + core for a in range(chips)] for core in range(2)]
        parts = [(rows - rows // 4, rows // 4), (0, rows - rows // 4)]
        summed = []
        for start, tall in parts:
            other_cot, other = results["other"]
            both = partials(c, start, tall, gate(cotangent), other_cot, tokens, other, rows)
            both = after(both)
            yield
            summed.append(
                lax.psum_scatter(
                    after(both), "fsdp", scatter_dimension=0, axis_index_groups=same_core, tiled=True
                )
            )
            yield
        hat, q = results["low_rank"]
        result = None
        for (start, _), part in zip(parts, summed):
            if result is None:
                result = begin(scale, start, part, feedback, hat, q)
            else:
                result = finish(scale, start, part, result)
            results["feedback"] = result
            yield

    def low_rank_chain():
        q_t = q_factor.T
        sent, factor = left_factor(scale, 1 - c, q_t, cotangent, tokens, rows, bf16)
        sent = after(sent)
        results["other"] = after(other_cot), after(other)
        results["sibling"] = after(results["sibling"])
        yield
        kept = left_kept(c + results["zero"], z, q_t, factor, tokens, feedback)
        reduction = split_sum(sent, kept, bf16)
        p_sum = yield from reduction
        p_all = yield from join(p_sum)
        p_own = lax.dynamic_slice_in_dim(p_all, (c * chips + z) * rows, rows, axis=1)
        z_part = right_part(scale, z, c, p_all, tokens, cotangent, feedback)
        reduction = split_sum(*z_part, f32)
        for _ in range(2):
            next(reduction)
            yield
        p_gated = gate(p_all)
        gram = dot(p_gated, p_gated, ((1,), (1,)))
        lower_factor = jnp.linalg.cholesky(gram)
        inverse = lax.linalg.triangular_solve(
            lower_factor, jnp.eye(gram.shape[0], dtype=f32), left_side=True, lower=True
        )
        inverse = after(inverse)
        yield
        z_sum = yield from finish_of(reduction)
        z_all = yield from join(z_sum)
        hat_own = dot(p_own.astype(f32), inverse, ((0,), (1,)), highest)
        q_next = dot(inverse, z_all, ((1,), (0,)), highest) / groups
        results["q_next"] = q_next.T
        results["low_rank"] = hat_own, q_next
        yield

    def own_weights():
        results["sibling"] = swap(weight, 1)
        yield
        pieces = [[weight[None]], [results["sibling"][None]]]
        results["own"], token = project(
            None, depth, gate(cotangent), pieces, jnp.stack([f, f ^ 1])[None]
        )
        results["zero"] = token[0, 0]
        yield

    def weights():
        share = rows // groups
        piece = lax.dynamic_slice_in_dim(weight, d * share, share, axis=0)
        near, across = [piece], [piece]
        for h in range(chips - 1):
            moves = [(a, a + 1) for a in range(h, chips - 1)]
            moves += [(a + 1, a) for a in range(chips - 1 - h)]
            from_near, from_across = near[-1], across[-1]
            near.append(paired(from_across, moves))
            across.append(paired(from_near, moves, 1))
            yield
            if 0 < h < chips - 2:
                near[-1], across[-1] = after(near[-1]), after(across[-1])
                yield
        near[-1] = after(near[-1])
        yield
        toward = jnp.where(z % 2 == 0, 1, -1)
        count = jnp.where(z % 2 == 0, chips - 1 - z, z)
        slots, sources = [], []
        for k in range(1, chips):
            slot = near[k]
            for m in range(1, k, 2):
                slot = jnp.where(count == m, across[k - m], slot)
            slots.append(slot)
            sources.append(jnp.where(k <= count, z + toward * k, z - toward * (k - count)))
        slots, far = after(jnp.stack(slots)), jnp.stack(sources)
        yield
        shares, twins = {0: [slots]}, {}
        middle = width // 2
        for m in range(1, groups):
            low_bit = m & -m
            high_bit = 1 << (m.bit_length() - 1)
            if low_bit == high_bit:
                source = shares[m ^ low_bit]
                shares[m] = [swap(x, low_bit * members) for x in source]
                if m == 1:
                    twins[0] = [swap(slots, 1)]
            else:
                first = jnp.concatenate(shares[m ^ low_bit], axis=2)[:, :, :middle]
                second = jnp.concatenate(shares[m ^ high_bit], axis=2)[:, :, middle:]
                yield
                shares[m] = [
                    swap(first, low_bit * members),
                    swap(second, high_bit * members),
                ]
        for m in range(groups):
            if m not in twins and len(shares[m]) == 1:
                twins[m] = [swap(x, 1) for x in shares[m]]
        yield
        for m in range(groups):
            if m not in twins:
                twins[m] = [swap(x, 1) for x in shares[m]]
        yield
        pieces, table = [], []
        for m in range(groups):
            for core, arrays in ((c, shares[m]), (1 - c, twins[m])):
                pieces.append(arrays)
                table.append((far * 2 + core) * groups + (d ^ m))
        results["input_grad"], _ = project(
            results["own"], depth, gate(cotangent), pieces, jnp.stack(table, axis=1)
        )
        yield

    chains = {"R": gradient(), "L": low_rank_chain(), "W": weights(), "O": own_weights()}
    order = "OWLWROWRWLLLRLWRWLLWLLLLWLLWLLW"
    for name in order:
        next(chains[name], None)
    for name in "LWR":
        for _ in chains[name]:
            pass
    return (results["input_grad"], results["q_next"], results["feedback"][None])


def solution(mesh):
    placed = (
        P(("dp", "fsdp"), None),
        P(("dp", "fsdp"), None),
        P("fsdp", None),
        P("dp", "fsdp", None),
        P(),
    )
    return jax.shard_map(
        per_device,
        mesh=mesh,
        in_specs=placed,
        out_specs=(P(("dp", "fsdp"), None), P(), P("dp", "fsdp", None)),
        check_vma=False,
    )
```
